32 devices in a mesh: chan: 8 (over z, y), tm: 4 (over x, core).
Axes of the slice: x: 2, y: 2, z: 4, core: 2. Of those that a mesh axis runs over, the one named last changes fastest.
Arguments:
- series: bfloat16 [4096, 3072], P('chan', 'tm'), may hold values from -6 to 6
- ref_list: int32 [8, 256], replicated, may hold values from 0 to 4095, as said below
Outputs:
- hankel: bfloat16 [128, 4096, 256], P('tm', 'chan')
The draws below stay inside these ranges and needn't reach their ends.
Inputs may be any that keep to these rules, and one draw needn't show every extreme that they name: `ref_list`: each row names 256 different channels. Over all rows together, exactly 32 different channels of each group's 512 channels (c // 512 equal) are named.
All inputs are finite; a program needn't handle non-finite values.
Results may differ from the reference program's by a relative error of at most 0.018.
Values may be sent and summed in bfloat16 or wider, within the bound.
No kernel may reach another device: no remote copies, remote signals or barrier semaphores. Data moves between devices by JAX's collectives and lax.ppermute only.
A program may use at most 128 MiB of HBM per device.

```python
import math
import jax
import jax.numpy as jnp
from jax import lax

CH = 4096
REFS = 256
LAGS = 128
TIME_DEV = 768
POOL_DEV = 32
GROUPS = 8
CHAN_DEV = 512
SAMPLES = 3072
N_TM = 4


def draw_ref_list(key, part):
    total_named = POOL_DEV * GROUPS
    first_key, second_key, third_key = jax.random.split(key, 3)
    offsets = jax.vmap(lambda sub_key: jax.random.permutation(sub_key, CHAN_DEV)[:POOL_DEV])(jax.random.split(first_key, GROUPS))
    candidates = (offsets + jnp.arange(GROUPS)[:, None] * CHAN_DEV).reshape(-1)
    shuffled = jax.random.permutation(second_key, total_named)
    positions = jax.vmap(lambda sub_key: jax.random.permutation(sub_key, REFS))(jax.random.split(third_key, GROUPS))
    picked = (jnp.arange(GROUPS)[:, None] * REFS + positions) % total_named
    return candidates[shuffled[picked]].astype(jnp.int32)


def block_scale(rng, dims, shards, low, largest):
    level = 1.0
    for axis_at, parts in shards:
        heights = jax.random.uniform(jax.random.fold_in(jax.random.fold_in(rng, 6), axis_at), (parts,), jnp.float32, low / len(shards), largest / len(shards))
        level = level * jnp.repeat(jnp.exp(heights), dims[axis_at] // parts).reshape((-1,) + (1,) * (len(dims) - 1 - axis_at))
    return level


def centred(own_key, extent, spread, limit, cuts=(), held_as=jnp.bfloat16):
    factor_of = block_scale(own_key, extent, cuts, -0.22, 0.18) if cuts else 1.0
    entries = jax.random.normal(own_key, extent, jnp.float32) * spread * factor_of
    return jnp.minimum(jnp.maximum(entries, -limit), limit).astype(held_as)


def setup_inputs(seed: int = 0) -> dict:
    seeds = jax.random.split(jax.random.key(seed), 3)
    series = centred(seeds[0], (CH, SAMPLES), 1.0, 6.0, ((0, 8), (1, 4)))
    ref_list = draw_ref_list(jax.random.fold_in(seeds[2], 71), 0)
    return {"series": series, "ref_list": ref_list}


def reference(series, ref_list):
    scale_factor = 1.0 / math.sqrt(SAMPLES)
    widened = jnp.concatenate([series, jnp.zeros((CH, LAGS), series.dtype)], axis=1).astype(jnp.float32)

    def per_group(group_index):
        group_rows = lax.dynamic_slice_in_dim(widened, group_index * CHAN_DEV, CHAN_DEV, 0)
        picked = jnp.take(widened[:, :SAMPLES], ref_list[group_index], axis=0)
        ref_blocks = picked.reshape(REFS, N_TM, TIME_DEV)

        def per_lag(lag_index):
            window = lax.dynamic_slice_in_dim(group_rows, lag_index, SAMPLES, 1).reshape(CHAN_DEV, N_TM, TIME_DEV)
            partials = jnp.einsum('cjt,rjt->jcr', window, ref_blocks, precision=lax.Precision.HIGHEST) * scale_factor
            partials = lax.optimization_barrier(partials.astype(jnp.bfloat16))
            return lax.optimization_barrier(jnp.sum(partials.astype(jnp.float32), axis=0))
        return lax.map(per_lag, jnp.arange(LAGS, dtype=jnp.int32))
    result = lax.map(per_group, jnp.arange(GROUPS, dtype=jnp.int32))
    return result.transpose(1, 0, 2, 3).reshape(LAGS, CH, REFS).astype(jnp.bfloat16)
```

```python
import functools
import math

import jax
import jax.numpy as jnp
from jax import lax
from jax.experimental import pallas as pl
from jax.experimental.pallas import tpu as pltpu
from jax.sharding import PartitionSpec as P

LAGS = 128
POOL = 32
BF16 = jnp.bfloat16
F32 = jnp.float32


def dot(a, b):
    return jnp.dot(a, b, preferred_element_type=F32)


def shifted(array, axis, by):
    size = lax.axis_size(axis)
    pairs = [(i, i + by) for i in range(size) if 0 <= i + by < size]
    return lax.ppermute(array, axis, pairs)


def lag_block(extended_rows, ref_block, first_lag, time_len, scale_factor):
    offsets = first_lag + jnp.arange(8, dtype=jnp.int32)
    windows = jax.vmap(lambda offset: lax.dynamic_slice_in_dim(extended_rows, offset, time_len, 1))(
        offsets
    )
    return (
        jnp.einsum("jct,rt->jcr", windows, ref_block, preferred_element_type=jnp.float32)
        * scale_factor
    )


def general_shards(series, ref_list):
    chan_rows, time_len = series.shape
    ref_count = ref_list.shape[1]
    group_index = lax.axis_index("chan")
    my_list = lax.dynamic_index_in_dim(ref_list, group_index, 0, keepdims=False)
    gathered_all = lax.all_gather(series, "chan", axis=0, tiled=True)
    ref_rows = jnp.take(gathered_all, my_list, axis=0)
    lag_tail = shifted(series[:, :LAGS], "tm", -1)
    extended = jnp.concatenate([series, lag_tail], axis=1)
    scale_factor = 1.0 / math.sqrt(time_len * lax.axis_size("tm"))
    lags_dev = LAGS // lax.axis_size("tm")

    def lag_step(carry, block_index):
        return (carry, lag_block(extended, ref_rows, 8 * block_index, time_len, scale_factor))

    _, stacked = lax.scan(
        lag_step, None, jnp.arange(lax.axis_size("tm") * lags_dev // 8, dtype=jnp.int32)
    )
    return lax.psum_scatter(
        stacked.reshape(lax.axis_size("tm") * lags_dev, chan_rows, ref_count).astype(jnp.bfloat16),
        "tm",
        scatter_dimension=0,
        tiled=True,
    )


def named_slots(list_ref, base, chan_rows):
    rows, width = list_ref.shape
    chan = base + lax.broadcasted_iota(jnp.int32, (chan_rows, 128), 0)
    hit = jnp.zeros((chan_rows, 128), jnp.bool_)
    for g in range(rows):
        for c in range(0, width, 128):
            hit = hit | (chan == list_ref[g : g + 1, c : c + 128])
    hits = jnp.where(hit, 1.0, 0.0).astype(BF16)
    named = jnp.where(dot(hits, jnp.ones((128, 128), BF16)) > 0.5, 1.0, 0.0)
    below = lax.broadcasted_iota(jnp.int32, (chan_rows, chan_rows), 1) < lax.broadcasted_iota(
        jnp.int32, (chan_rows, chan_rows), 0
    )
    rank = dot(jnp.where(below, 1.0, 0.0).astype(BF16), named.astype(BF16))
    slot = lax.broadcasted_iota(jnp.int32, (chan_rows, 128), 1).astype(F32)
    return jnp.where(rank == slot, named, 0.0)


def select_kernel(group_ref, list_ref, s_ref, pool_ref):
    chan_rows = s_ref.shape[0]
    picks = named_slots(list_ref, group_ref[0] * chan_rows, chan_rows)
    pool_ref[...] = dot(picks.T[:POOL].astype(BF16), s_ref[...]).astype(BF16)


def order_kernel(group_ref, list_ref, mine_ref, order_ref, *, chan_rows):
    width = mine_ref.shape[1]

    @pl.loop(0, order_ref.shape[0] // POOL)
    def _(d):
        base = (group_ref[0] ^ d) * chan_rows
        picks = named_slots(list_ref, base, chan_rows)
        chan = base + lax.broadcasted_iota(jnp.int32, (chan_rows, width), 0)
        wanted = jnp.where(chan == mine_ref[...], 1.0, 0.0).astype(BF16)
        rows = pl.ds(pl.multiple_of(d * POOL, POOL), POOL)
        order_ref[rows, :] = dot(picks.T[:POOL].astype(BF16), wanted).astype(BF16)


PH = 16
WIN = 512
COMBOS = ((0, 0), (1, 0), (1, 4), (2, 0), (3, 0), (3, 4), (2, 8), (3, 8), (3, 12))


def corr_kernel(tm_ref, order_ref, *refs, time_len, n_tm, n_pool, scale):
    pieces = refs[: n_tm + n_pool]
    out_ref, s_raw, r_raw, xf, s9, rv, sem_s, sem_r = refs[n_tm + n_pool :]
    me = tm_ref[0]
    total = s_raw.shape[1]
    windows = total // WIN
    per = WIN // PH
    quarter = WIN // 4

    @pl.when(pl.program_id(0) == 0)
    def _():
        def s_copy(e):
            lanes = pl.ds(pl.multiple_of((me ^ e) * time_len, 128), time_len)
            return pltpu.make_async_copy(pieces[e], s_raw.at[:, lanes], sem_s.at[e])

        def r_copy(d, c, x):
            lanes = pl.ds(pl.multiple_of((me ^ (c + 2 * x)) * time_len, 128), time_len)
            return pltpu.make_async_copy(
                pieces[n_tm + 2 * d + c].at[POOL * x : POOL * (x + 1)],
                r_raw.at[POOL * d : POOL * (d + 1), lanes],
                sem_r.at[d, c, x],
            )

        r_copies = [r_copy(d, c, x) for d in range(n_pool // 2) for c in range(2) for x in range(2)]
        s_copies = [s_copy(e) for e in range(n_tm)]
        for copy in r_copies + s_copies:
            copy.start()
        for copy in r_copies:
            copy.wait()

        at = lax.broadcasted_iota(jnp.int32, (256, 256), 0)
        to = lax.broadcasted_iota(jnp.int32, (256, 256), 1)
        turn = jnp.where(to == PH * (at & 15) + (at >> 4), 1.0, 0.0).astype(BF16)
        for h in range(2):
            for p in range(PH):
                xf[h, p, 0:8, :] = jnp.zeros((8, 128), F32)

        @pl.loop(0, total // 256)
        def _(b):
            block = r_raw[:, pl.ds(pl.multiple_of(b * 256, 256), 256)]
            turned = lax.dot_general(
                turn, block, (((1,), (1,)), ((), ())), preferred_element_type=F32
            ).astype(BF16)
            placed = dot(turned, order_ref[...])
            for p in range(PH):
                for h in range(2):
                    xf[h, p, pl.ds(pl.multiple_of(8 + 16 * b, 8), 16), :] = placed[
                        16 * p : 16 * p + 16, 128 * h : 128 * h + 128
                    ]

        @pl.loop(0, 35)
        def _(idx):
            k = idx - 31

            def rows(kk, b, h):
                level = kk >> 4
                return xf[h, kk & 15, pl.ds(8 + per * b + level - 2 * me, per), :]

            here = pl.ds(pl.multiple_of(idx * per, per), per)
            for b in range(windows):
                for h in range(2):
                    x0, x4, x8, x12 = (rows(k + o, b, h) for o in (0, 4, 8, 12))
                    lanes = slice(128 * h, 128 * h + 128)
                    f0, f8 = x4 - x0, x12 - x8
                    rv[0, b, here, lanes] = x0.astype(BF16)
                    rv[1, b, here, lanes] = f0.astype(BF16)
                    rv[2, b, here, lanes] = (x8 - x0).astype(BF16)
                    rv[3, b, here, lanes] = (f8 - f0).astype(BF16)

        for copy in s_copies:
            copy.wait()
        at = lax.broadcasted_iota(jnp.int32, (WIN, WIN), 0)
        to = lax.broadcasted_iota(jnp.int32, (WIN, WIN), 1)
        turn = jnp.where(at == PH * (to & (per - 1)) + to // per, 1.0, 0.0).astype(BF16)

        @pl.loop(0, windows)
        def _(b):
            window = s_raw[:, pl.ds(pl.multiple_of(b * WIN, WIN), WIN)]
            turned = dot(window, turn)
            t = [turned[:, quarter * g : quarter * (g + 1)] for g in range(4)]
            u0, u1 = t[0] + t[2], t[1] + t[3]
            sums = (u0 + u1, u1, -u0, t[2] + t[3], t[3], -t[2], -(t[0] + t[1]), -t[1], t[0])
            lanes = pl.ds(pl.multiple_of(b * quarter, quarter), quarter)
            for i, value in enumerate(sums):
                s9[i, :, lanes] = value.astype(BF16)

    step = pl.program_id(0)
    first = 31 - 16 * (step >> 2) - (step & 3)

    def product(i):
        v, off = COMBOS[i]
        rows = pl.ds(pl.multiple_of((first - off) * per, per), 4 * per)
        slab = jnp.concatenate([rv[v, b, rows, :] for b in range(windows)], axis=0)
        return dot(s9[i], slab)

    p = [product(i) for i in range(9)]
    for at, parts in enumerate(((0, 1, 3, 4), (0, 2, 3, 5), (0, 1, 6, 7), (0, 2, 6, 8))):
        out_ref[0, at, 0] = (scale * sum([p[i] for i in parts[1:]], p[parts[0]])).astype(BF16)


def flip(array, axis, by):
    return lax.ppermute(array, axis, [(i, i ^ by) for i in range(lax.axis_size(axis))])


def block_shards(series, ref_list):
    chan_rows, time_len = series.shape
    groups, refs = ref_list.shape
    n_tm = lax.axis_size("tm")
    total = time_len * n_tm
    lags_dev = LAGS // n_tm
    group = lax.axis_index("chan").astype(jnp.int32)
    smem = pl.BlockSpec(memory_space=pltpu.SMEM)
    vmem = pl.BlockSpec(memory_space=pltpu.VMEM)
    hbm = pl.BlockSpec(memory_space=pl.ANY)
    big = pltpu.CompilerParams(vmem_limit_bytes=58 * 2**20)
    own_pool = pl.pallas_call(
        select_kernel,
        in_specs=[smem, vmem, vmem],
        out_specs=vmem,
        out_shape=jax.ShapeDtypeStruct((POOL, time_len), BF16),
    )(group[None], ref_list, series)
    pool_x = flip(own_pool, "tm", 2)
    series_x = flip(series, "tm", 2)
    series_c = flip(series, "tm", 1)
    series_xc = flip(series_x, "tm", 1)
    mine = lax.dynamic_slice_in_dim(ref_list, group, 1, 0)
    order = pl.pallas_call(
        functools.partial(order_kernel, chan_rows=chan_rows),
        in_specs=[smem, vmem, vmem],
        out_specs=vmem,
        out_shape=jax.ShapeDtypeStruct((groups * POOL, refs), BF16),
        cost_estimate=pl.CostEstimate(flops=10**9, bytes_accessed=10**6, transcendentals=0),
    )(group[None], ref_list, mine)
    pair = jnp.concatenate([own_pool, pool_x], axis=0)
    along_z = [pair] + [flip(pair, "chan", 2 * d) for d in range(1, groups // 2)]
    pool = []
    for piece in along_z:
        pool += [piece, flip(piece, "chan", 1)]
    pieces = []
    for piece in pool:
        pieces += [piece, flip(piece, "tm", 1)]
    n_pool = len(pieces)
    windows = total // WIN
    out = pl.pallas_call(
        functools.partial(
            corr_kernel, time_len=time_len, n_tm=n_tm, n_pool=n_pool, scale=1.0 / math.sqrt(total)
        ),
        grid=(8,),
        in_specs=[smem, pl.BlockSpec((groups * POOL, refs), lambda i: (0, 0))] + [hbm] * (n_tm + n_pool),
        out_specs=pl.BlockSpec((1, 4, 1, chan_rows, refs), lambda i: (i // 4, 0, i % 4, 0, 0)),
        out_shape=jax.ShapeDtypeStruct((2, 4, 4, chan_rows, refs), BF16),
        scratch_shapes=[
            pltpu.VMEM((chan_rows, total), BF16),
            pltpu.VMEM((groups * POOL, total), BF16),
            pltpu.VMEM((2, PH, total // PH + 8, 128), F32),
            pltpu.VMEM((9, chan_rows, total // 4), BF16),
            pltpu.VMEM((4, windows, 35 * (WIN // PH), refs), BF16),
            pltpu.SemaphoreType.DMA((n_tm,)),
            pltpu.SemaphoreType.DMA((n_pool // 2, 2, 2)),
        ],
        compiler_params=big,
        cost_estimate=pl.CostEstimate(flops=15 * 10**9, bytes_accessed=2 * 10**7, transcendentals=0),
    )(lax.axis_index("tm").astype(jnp.int32)[None], order, series, series_c, series_x, series_xc, *pieces)
    return out.reshape(lags_dev, chan_rows, refs)


def solution(mesh):
    in_specs = (P("chan", "tm"), P())
    out_specs = P("tm", "chan", None)
    sizes = (mesh.shape["chan"], mesh.shape["tm"])
    body = block_shards if sizes == (8, 4) else general_shards
    return jax.shard_map(body, mesh=mesh, in_specs=in_specs, out_specs=out_specs, check_vma=False)
```

```python
import functools
import math

import jax
import jax.numpy as jnp
from jax import lax
from jax.experimental import pallas as pl
from jax.experimental.pallas import tpu as pltpu
from jax.sharding import PartitionSpec as P

LAGS = 128
POOL = 32
BF16 = jnp.bfloat16
F32 = jnp.float32


def dot(a, b):
    return jnp.dot(a, b, preferred_element_type=F32)


def shifted(array, axis, by):
    size = lax.axis_size(axis)
    pairs = [(i, i + by) for i in range(size) if 0 <= i + by < size]
    return lax.ppermute(array, axis, pairs)


def lag_block(extended_rows, ref_block, first_lag, time_len, scale_factor):
    offsets = first_lag + jnp.arange(8, dtype=jnp.int32)
    windows = jax.vmap(lambda offset: lax.dynamic_slice_in_dim(extended_rows, offset, time_len, 1))(
        offsets
    )
    return (
        jnp.einsum("jct,rt->jcr", windows, ref_block, preferred_element_type=jnp.float32)
        * scale_factor
    )


def general_shards(series, ref_list):
    chan_rows, time_len = series.shape
    ref_count = ref_list.shape[1]
    group_index = lax.axis_index("chan")
    my_list = lax.dynamic_index_in_dim(ref_list, group_index, 0, keepdims=False)
    gathered_all = lax.all_gather(series, "chan", axis=0, tiled=True)
    ref_rows = jnp.take(gathered_all, my_list, axis=0)
    lag_tail = shifted(series[:, :LAGS], "tm", -1)
    extended = jnp.concatenate([series, lag_tail], axis=1)
    scale_factor = 1.0 / math.sqrt(time_len * lax.axis_size("tm"))
    lags_dev = LAGS // lax.axis_size("tm")

    def lag_step(carry, block_index):
        return (carry, lag_block(extended, ref_rows, 8 * block_index, time_len, scale_factor))

    _, stacked = lax.scan(
        lag_step, None, jnp.arange(lax.axis_size("tm") * lags_dev // 8, dtype=jnp.int32)
    )
    return lax.psum_scatter(
        stacked.reshape(lax.axis_size("tm") * lags_dev, chan_rows, ref_count).astype(jnp.bfloat16),
        "tm",
        scatter_dimension=0,
        tiled=True,
    )


def ones_where(condition):
    return jnp.where(condition, 1.0, 0.0).astype(BF16)


def iota(shape, dim):
    return lax.broadcasted_iota(jnp.int32, shape, dim)


def nt_dot(a, b):
    return lax.dot_general(a, b, (((1,), (1,)), ((), ())), preferred_element_type=F32)


def marks_of(list_ref, highs):
    groups, width = list_ref.shape
    rows = [list_ref[g : g + 1, c : c + 128] for g in range(groups) for c in range(0, width, 128)]
    high = jnp.concatenate([ones_where(iota((highs, 128), 0) == (row >> 7)) for row in rows], axis=1)
    low = jnp.concatenate([ones_where(iota((128, 128), 0) == (row & 127)) for row in rows], axis=1)
    return high, low


def select_kernel(group_ref, list_ref, s_hbm, pool_ref, pair_ref, s_ref, rank_ref, sem):
    copy = pltpu.make_async_copy(s_hbm, s_ref, sem)
    copy.start()
    per = s_ref.shape[0] // 128
    highs = list_ref.shape[0] * per
    high, low = marks_of(list_ref, highs)
    named = nt_dot(high, low) > 0.5
    marks = ones_where(named)
    before = ones_where(iota((128, 128), 0) < iota((128, 128), 1))
    held = dot(marks, jnp.ones((128, 128), BF16)).astype(BF16)
    h_to, h_from = iota((highs, highs), 0), iota((highs, highs), 1)
    earlier = ones_where((h_to // per == h_from // per) & (h_from < h_to))
    rank_ref[...] = jnp.where(named, dot(marks, before) + dot(earlier, held), -1.0)
    slot = iota((POOL, 128), 0).astype(F32)
    picks = [
        ones_where(jnp.broadcast_to(rank_ref[pl.ds(group_ref[0] * per + h, 1), :], (POOL, 128)) == slot)
        for h in range(per)
    ]
    copy.wait()
    rows = dot(jnp.concatenate(picks, axis=1), s_ref[...]).astype(BF16)
    pool_ref[...] = rows
    pair_ref[:POOL] = rows
    pair_ref[POOL:] = jnp.zeros_like(rows)


def order_kernel(group_ref, list_ref, pool_ref, order_ref, *, per):
    del pool_ref
    groups, width = list_ref.shape
    highs = groups * per
    own = group_ref[0]
    high, low = marks_of(list_ref, highs)
    marks = ones_where(nt_dot(low, high) > 0.5)
    after = ones_where(iota((128, 128), 1) < iota((128, 128), 0))
    held = dot(jnp.ones((128, 128), BF16), marks).astype(BF16)
    h_from, h_to = iota((highs, highs), 0), iota((highs, highs), 1)
    earlier = ones_where((h_to // per == h_from // per) & (h_from < h_to))
    rank = dot(after, marks) + dot(held, earlier)
    place = rank + (POOL * ((iota((128, highs), 1) // per) ^ own)).astype(F32)
    mine = list_ref[pl.ds(own, 1), :]
    mine_high = ones_where(iota((highs, width), 0) == (mine >> 7))
    mine_low = jnp.where(iota((128, width), 0) == (mine & 127), 1.0, 0.0)
    at = jnp.sum(dot(place.astype(BF16), mine_high) * mine_low, axis=0, keepdims=True)
    order_ref[...] = ones_where(iota(order_ref.shape, 0).astype(F32) == at)


PH = 16
WIN = 512
PER = WIN // PH
QUARTER = WIN // 4
COMBOS = ((0, 0), (1, 0), (1, 4), (2, 0), (3, 0), (3, 4), (2, 8), (3, 8), (3, 12))


def series_kernel(core_ref, mine_ref, other_ref, out_ref, raw, sem):
    time_len = mine_ref.shape[1]
    copies = [
        pltpu.make_async_copy(
            ref, raw.at[:, pl.ds(pl.multiple_of((core_ref[0] ^ e) * time_len, 128), time_len)], sem.at[e]
        )
        for e, ref in enumerate((mine_ref, other_ref))
    ]
    for copy in copies:
        copy.start()
    at, to = iota((WIN, WIN), 0), iota((WIN, WIN), 1)
    turn = ones_where(at == PH * (to & (PER - 1)) + to // PER)
    for copy in copies:
        copy.wait()
    for b in range(raw.shape[1] // WIN):
        turned = dot(raw[:, b * WIN : (b + 1) * WIN], turn)
        t = [turned[:, QUARTER * g : QUARTER * (g + 1)] for g in range(4)]
        u0, u1 = t[0] + t[2], t[1] + t[3]
        sums = (u0 + u1, u1, -u0, t[2] + t[3], t[3], -t[2], -(t[0] + t[1]), -t[1], t[0])
        for i, value in enumerate(sums):
            out_ref[i, :, b * QUARTER : (b + 1) * QUARTER] = value.astype(BF16)


def corr_kernel(tm_ref, order_ref, *refs, n_pool, time_len, scale):
    halves = refs[:2]
    pieces = refs[2 : 2 + n_pool]
    out_ref, r_raw, xf, xr, rv0, rv1, sem_r = refs[2 + n_pool :]
    me = tm_ref[0]
    total = r_raw.shape[1]
    windows = total // WIN
    half_w = windows // 2
    step = pl.program_id(0)

    def slab(idx):
        return pl.ds(pl.multiple_of(idx * PER, PER), PER)

    def make(idx, rv, base, which):
        for b in range(windows):
            x0, x4, x8, x12 = (xr[b, slab(idx + o), :].astype(F32) for o in (0, 4, 8, 12))
            f0 = x4 - x0
            if 0 in which:
                rv[0, b, slab(idx - base), :] = f0.astype(BF16)
            if 1 in which:
                rv[1, b, slab(idx - base), :] = (x8 - x0).astype(BF16)
            rv[2, b, slab(idx - base), :] = ((x12 - x8) - f0).astype(BF16)

    @pl.when(step == 0)
    def _():
        def r_copy(d, c, x):
            lanes = pl.ds(pl.multiple_of((me ^ (c + 2 * x)) * time_len, 128), time_len)
            return pltpu.make_async_copy(
                pieces[2 * d + c].at[POOL * x : POOL * (x + 1)],
                r_raw.at[POOL * d : POOL * (d + 1), lanes],
                sem_r.at[d, c, x],
            )

        r_copies = [r_copy(d, c, x) for d in range(n_pool // 2) for c in range(2) for x in range(2)]
        for copy in r_copies:
            copy.start()
        at, to = iota((256, 256), 0), iota((256, 256), 1)
        turn = ones_where(to == PH * (at & 15) + (at >> 4))
        for h in range(2):
            for p in range(PH):
                xf[h, p, 0:8, :] = jnp.zeros((8, 128), F32)
        for copy in r_copies:
            copy.wait()
        for b in range(total // 256):
            turned = nt_dot(turn, r_raw[:, b * 256 : (b + 1) * 256]).astype(BF16)
            placed = dot(turned, order_ref[...])
            for p in range(PH):
                for h in range(2):
                    xf[h, p, 8 + 16 * b : 24 + 16 * b, :] = placed[
                        16 * p : 16 * p + 16, 128 * h : 128 * h + 128
                    ]

        @pl.loop(0, 47)
        def _(idx):
            k = idx - 31
            for b in range(windows):
                half = (me >> 1) ^ (b // half_w)
                row = 8 + PER * (half_w * half + b % half_w) + (k >> 4) - 2 * me
                for h in range(2):
                    xr[b, slab(idx), 128 * h : 128 * h + 128] = xf[h, k & 15, pl.ds(row, PER), :].astype(BF16)

        for low, high, which in ((24, 35, (0, 1)), (20, 24, (1,)), (16, 20, ())):

            @pl.loop(low, high)
            def _(idx):
                make(idx, rv0, 16, which)

    def products(rv):
        first = 15 - (step & 3)

        def product(i):
            v, off = COMBOS[i]
            if v == 0:
                rows = pl.ds(pl.multiple_of((first + 16 - 16 * (step >> 2)) * PER, PER), 4 * PER)
                parts = [xr[b, rows, :] for b in range(windows)]
            else:
                rows = pl.ds(pl.multiple_of((first - off) * PER, PER), 4 * PER)
                parts = [rv[v - 1, b, rows, :] for b in range(windows)]
            return dot(jnp.concatenate([half[i] for half in halves], axis=1), jnp.concatenate(parts, axis=0))

        p = [product(i) for i in range(9)]
        w0, w1 = p[0] + p[3], p[0] + p[6]
        for at, value in enumerate((w0 + (p[1] + p[4]), w0 + (p[2] + p[5]), w1 + (p[1] + p[7]), w1 + (p[2] + p[8]))):
            out_ref[0, at, 0] = (scale * value).astype(BF16)

    @pl.when(step < 4)
    def _():
        products(rv0)
        for o in range(5):
            make(jnp.maximum(18 - 5 * step - o, 0), rv1, 0, (0, 1))

    @pl.when(step >= 4)
    def _():
        products(rv1)


def flip(array, axis, by):
    return lax.ppermute(array, axis, [(i, i ^ by) for i in range(lax.axis_size(axis))])


def after(array, *others):
    return lax.optimization_barrier((array, *others))[0]


def block_shards(series, ref_list):
    chan_rows, time_len = series.shape
    groups, refs = ref_list.shape
    n_tm = lax.axis_size("tm")
    total = time_len * n_tm
    lags_dev = LAGS // n_tm
    group = lax.axis_index("chan").astype(jnp.int32)
    me = lax.axis_index("tm").astype(jnp.int32)
    smem = pl.BlockSpec(memory_space=pltpu.SMEM)
    vmem = pl.BlockSpec(memory_space=pltpu.VMEM)
    hbm = pl.BlockSpec(memory_space=pltpu.HBM)
    anywhere = pl.BlockSpec(memory_space=pl.ANY)
    own_pool, pair = pl.pallas_call(
        select_kernel,
        in_specs=[smem, vmem, hbm],
        out_specs=[vmem, vmem],
        out_shape=[jax.ShapeDtypeStruct((rows, time_len), BF16) for rows in (POOL, 2 * POOL)],
        scratch_shapes=[
            pltpu.VMEM((chan_rows, time_len), BF16),
            pltpu.VMEM((groups * chan_rows // 128, 128), F32),
            pltpu.SemaphoreType.DMA(()),
        ],
    )(group[None], ref_list, series)
    pool_x = flip(own_pool, "tm", 2)
    order = pl.pallas_call(
        functools.partial(order_kernel, per=chan_rows // 128),
        in_specs=[smem, vmem, hbm],
        out_specs=vmem,
        out_shape=jax.ShapeDtypeStruct((groups * POOL, refs), BF16),
        cost_estimate=pl.CostEstimate(flops=10**9, bytes_accessed=10**6, transcendentals=0),
    )(group[None], ref_list, own_pool)
    pair = lax.dynamic_update_slice(after(pair, order), pool_x, (POOL, 0))
    series_x = flip(after(series, pool_x), "tm", 2)
    along_z = [pair] + [flip(pair, "chan", 2 * d) for d in range(1, groups // 2)]
    pool = []
    for piece in along_z:
        pool += [piece, flip(piece, "chan", 1)]
    series_c = flip(after(series, *along_z), "tm", 1)
    series_xc = flip(after(series_x, *pool), "tm", 1)

    def phases(mine, other):
        return pl.pallas_call(
            series_kernel,
            in_specs=[smem, hbm, hbm],
            out_specs=vmem,
            out_shape=jax.ShapeDtypeStruct((9, chan_rows, time_len // 2), BF16),
            scratch_shapes=[pltpu.VMEM((chan_rows, 2 * time_len), BF16), pltpu.SemaphoreType.DMA((2,))],
            compiler_params=pltpu.CompilerParams(vmem_limit_bytes=16 * 2**20),
            cost_estimate=pl.CostEstimate(
                flops=4 * chan_rows * time_len * WIN, bytes_accessed=6 * 10**6, transcendentals=0
            ),
        )((me & 1)[None], mine, other)

    halves = [phases(series, series_c), phases(series_x, series_xc)]
    pieces = []
    for piece in pool:
        pieces += [piece, flip(piece, "tm", 1)]
    n_pool = len(pieces)
    windows = total // WIN
    out = pl.pallas_call(
        functools.partial(corr_kernel, time_len=time_len, n_pool=n_pool, scale=1.0 / math.sqrt(total)),
        grid=(8,),
        in_specs=[smem, pl.BlockSpec((groups * POOL, refs), lambda i: (0, 0))] + [vmem] * 2 + [hbm] * n_pool,
        out_specs=pl.BlockSpec((1, 4, 1, chan_rows, refs), lambda i: (i // 4, 0, i % 4, 0, 0)),
        out_shape=jax.ShapeDtypeStruct((2, 4, 4, chan_rows, refs), BF16),
        scratch_shapes=[
            pltpu.VMEM((groups * POOL, total), BF16),
            pltpu.VMEM((2, PH, total // PH + 8, 128), F32),
            pltpu.VMEM((windows, 47 * PER, refs), BF16),
            pltpu.VMEM((3, windows, 19 * PER, refs), BF16),
            pltpu.VMEM((3, windows, 19 * PER, refs), BF16),
            pltpu.SemaphoreType.DMA((n_pool // 2, 2, 2)),
        ],
        compiler_params=pltpu.CompilerParams(vmem_limit_bytes=40 * 2**20),
        cost_estimate=pl.CostEstimate(flops=15 * 10**9, bytes_accessed=2 * 10**7, transcendentals=0),
    )(me[None], order, *halves, *pieces)
    return out.reshape(lags_dev, chan_rows, refs)


def solution(mesh):
    in_specs = (P("chan", "tm"), P())
    out_specs = P("tm", "chan", None)
    sizes = (mesh.shape["chan"], mesh.shape["tm"])
    body = block_shards if sizes == (8, 4) else general_shards
    return jax.shard_map(body, mesh=mesh, in_specs=in_specs, out_specs=out_specs, check_vma=False)
```

```python
import functools
import math

import jax
import jax.numpy as jnp
from jax import lax
from jax.experimental import pallas as pl
from jax.experimental.pallas import tpu as pltpu
from jax.sharding import PartitionSpec as P

LAGS = 128
POOL = 32
BF16 = jnp.bfloat16
F32 = jnp.float32


def dot(a, b):
    return jnp.dot(a, b, preferred_element_type=F32)


def shifted(array, axis, by):
    size = lax.axis_size(axis)
    pairs = [(i, i + by) for i in range(size) if 0 <= i + by < size]
    return lax.ppermute(array, axis, pairs)


def lag_block(extended_rows, ref_block, first_lag, time_len, scale_factor):
    offsets = first_lag + jnp.arange(8, dtype=jnp.int32)
    windows = jax.vmap(lambda offset: lax.dynamic_slice_in_dim(extended_rows, offset, time_len, 1))(
        offsets
    )
    return (
        jnp.einsum("jct,rt->jcr", windows, ref_block, preferred_element_type=jnp.float32)
        * scale_factor
    )


def general_shards(series, ref_list):
    chan_rows, time_len = series.shape
    ref_count = ref_list.shape[1]
    group_index = lax.axis_index("chan")
    my_list = lax.dynamic_index_in_dim(ref_list, group_index, 0, keepdims=False)
    gathered_all = lax.all_gather(series, "chan", axis=0, tiled=True)
    ref_rows = jnp.take(gathered_all, my_list, axis=0)
    lag_tail = shifted(series[:, :LAGS], "tm", -1)
    extended = jnp.concatenate([series, lag_tail], axis=1)
    scale_factor = 1.0 / math.sqrt(time_len * lax.axis_size("tm"))
    lags_dev = LAGS // lax.axis_size("tm")

    def lag_step(carry, block_index):
        return (carry, lag_block(extended, ref_rows, 8 * block_index, time_len, scale_factor))

    _, stacked = lax.scan(
        lag_step, None, jnp.arange(lax.axis_size("tm") * lags_dev // 8, dtype=jnp.int32)
    )
    return lax.psum_scatter(
        stacked.reshape(lax.axis_size("tm") * lags_dev, chan_rows, ref_count).astype(jnp.bfloat16),
        "tm",
        scatter_dimension=0,
        tiled=True,
    )


def ones_where(condition):
    return jnp.where(condition, 1.0, 0.0).astype(BF16)


def iota(shape, dim):
    return lax.broadcasted_iota(jnp.int32, shape, dim)


def nt_dot(a, b):
    return lax.dot_general(a, b, (((1,), (1,)), ((), ())), preferred_element_type=F32)


def marks_of(list_ref, highs):
    groups, width = list_ref.shape
    rows = [list_ref[g : g + 1, c : c + 128] for g in range(groups) for c in range(0, width, 128)]
    high = jnp.concatenate([ones_where(iota((highs, 128), 0) == (row >> 7)) for row in rows], axis=1)
    low = jnp.concatenate([ones_where(iota((128, 128), 0) == (row & 127)) for row in rows], axis=1)
    return high, low


def select_kernel(group_ref, list_ref, s_hbm, pool_ref, pair_ref, s_ref, rank_ref, sem):
    copy = pltpu.make_async_copy(s_hbm, s_ref, sem)
    copy.start()
    per = s_ref.shape[0] // 128
    highs = list_ref.shape[0] * per
    high, low = marks_of(list_ref, highs)
    named = nt_dot(high, low) > 0.5
    marks = ones_where(named)
    before = ones_where(iota((128, 128), 0) < iota((128, 128), 1))
    held = dot(marks, jnp.ones((128, 128), BF16)).astype(BF16)
    h_to, h_from = iota((highs, highs), 0), iota((highs, highs), 1)
    earlier = ones_where((h_to // per == h_from // per) & (h_from < h_to))
    rank_ref[...] = jnp.where(named, dot(marks, before) + dot(earlier, held), -1.0)
    slot = iota((POOL, 128), 0).astype(F32)
    picks = [
        ones_where(jnp.broadcast_to(rank_ref[pl.ds(group_ref[0] * per + h, 1), :], (POOL, 128)) == slot)
        for h in range(per)
    ]
    copy.wait()
    rows = dot(jnp.concatenate(picks, axis=1), s_ref[...]).astype(BF16)
    pool_ref[...] = rows
    pair_ref[:POOL] = rows
    pair_ref[POOL:] = jnp.zeros_like(rows)


def order_kernel(group_ref, list_ref, pool_ref, order_ref, *, per):
    del pool_ref
    groups, width = list_ref.shape
    highs = groups * per
    own = group_ref[0]
    high, low = marks_of(list_ref, highs)
    marks = ones_where(nt_dot(low, high) > 0.5)
    after = ones_where(iota((128, 128), 1) < iota((128, 128), 0))
    held = dot(jnp.ones((128, 128), BF16), marks).astype(BF16)
    h_from, h_to = iota((highs, highs), 0), iota((highs, highs), 1)
    earlier = ones_where((h_to // per == h_from // per) & (h_from < h_to))
    rank = dot(after, marks) + dot(held, earlier)
    place = rank + (POOL * ((iota((128, highs), 1) // per) ^ own)).astype(F32)
    mine = list_ref[pl.ds(own, 1), :]
    mine_high = ones_where(iota((highs, width), 0) == (mine >> 7))
    mine_low = jnp.where(iota((128, width), 0) == (mine & 127), 1.0, 0.0)
    at = jnp.sum(dot(place.astype(BF16), mine_high) * mine_low, axis=0, keepdims=True)
    order_ref[...] = ones_where(iota(order_ref.shape, 0).astype(F32) == at)


PH = 16
WIN = 512
PER = WIN // PH
QUARTER = WIN // 4
COMBOS = ((0, 0), (1, 0), (1, 4), (2, 0), (3, 0), (3, 4), (2, 8), (3, 8), (3, 12))


def series_kernel(core_ref, mine_ref, other_ref, out_ref, raw, sem):
    time_len = mine_ref.shape[1]
    copies = [
        pltpu.make_async_copy(
            ref, raw.at[:, pl.ds(pl.multiple_of((core_ref[0] ^ e) * time_len, 128), time_len)], sem.at[e]
        )
        for e, ref in enumerate((mine_ref, other_ref))
    ]
    for copy in copies:
        copy.start()
    at, to = iota((WIN, WIN), 0), iota((WIN, WIN), 1)
    turn = ones_where(at == PH * (to & (PER - 1)) + to // PER)
    for copy in copies:
        copy.wait()
    for b in range(raw.shape[1] // WIN):
        turned = dot(raw[:, b * WIN : (b + 1) * WIN], turn)
        t = [turned[:, QUARTER * g : QUARTER * (g + 1)] for g in range(4)]
        u0, u1 = t[0] + t[2], t[1] + t[3]
        sums = (u0 + u1, u1, -u0, t[2] + t[3], t[3], -t[2], -(t[0] + t[1]), -t[1], t[0])
        for i, value in enumerate(sums):
            out_ref[i, :, b * QUARTER : (b + 1) * QUARTER] = value.astype(BF16)


def refs_kernel(order_ref, *refs):
    *pieces, out_ref = refs
    time_len = pieces[0].shape[1]
    at, to = iota((256, 256), 0), iota((256, 256), 1)
    turn = ones_where(to == PH * (at & 15) + (at >> 4))
    blocks = [(x, b) for x in range(2) for b in range(time_len // 256)]
    turned = []
    for x, b in blocks:
        block = [piece[POOL * x : POOL * (x + 1), 256 * b : 256 * (b + 1)] for piece in pieces]
        turned.append(nt_dot(turn, jnp.concatenate(block, axis=0)).astype(BF16))
    placed = dot(jnp.concatenate(turned, axis=0), order_ref[...]).astype(BF16)
    for i, (x, b) in enumerate(blocks):
        for p in range(PH):
            out_ref[x, p, 16 * b : 16 * (b + 1), :] = placed[256 * i + 16 * p : 256 * i + 16 * (p + 1)]


def corr_kernel(tm_ref, mine_ref, other_ref, *refs, windows, scale):
    halves = refs[:2]
    out_ref, xf, xr, rv0, rv1 = refs[2:]
    me = tm_ref[0]
    half_w = windows // 2
    step = pl.program_id(0)

    def slab(idx):
        return pl.ds(pl.multiple_of(idx * PER, PER), PER)

    def make(idx, rv, base, which, windows_of):
        for b in windows_of:
            x0, x4, x8, x12 = (xr[b, slab(idx + o), :] for o in (0, 4, 8, 12))
            f0 = x4 - x0
            if 0 in which:
                rv[0, b, slab(idx - base), :] = f0
            if 1 in which:
                rv[1, b, slab(idx - base), :] = x8 - x0
            rv[2, b, slab(idx - base), :] = (x12 - x8) - f0

    @pl.when(step == 0)
    def _():
        block_rows = mine_ref.shape[2]
        for h in range(2):
            lanes = slice(128 * h, 128 * h + 128)
            for p in range(PH):
                xf[h, p, 0:8, :] = jnp.zeros((8, 128), F32)
                for c, ref in enumerate((mine_ref, other_ref)):
                    for x in range(2):
                        row = pl.multiple_of(8 + block_rows * (me ^ (c + 2 * x)), 8)
                        xf[h, p, pl.ds(row, block_rows), :] = ref[x, p, :, lanes].astype(F32)

        @pl.loop(0, 47)
        def _(idx):
            k = idx - 31
            for b in range(windows):
                half = (me >> 1) ^ (b // half_w)
                row = 8 + PER * (half_w * half + b % half_w) + (k >> 4) - 2 * me
                for h in range(2):
                    xr[b, slab(idx), 128 * h : 128 * h + 128] = xf[h, k & 15, pl.ds(row, PER), :].astype(BF16)

        for low, high, which in ((24, 35, (0, 1)), (20, 24, (1,)), (16, 20, ())):

            @pl.loop(low, high)
            def _(idx):
                make(idx, rv0, 16, which, range(windows))

    def products(rv, beside):
        first = 15 - (step & 3)

        def product(i):
            v, off = COMBOS[i]
            if v == 0:
                rows = pl.ds(pl.multiple_of((first + 16 - 16 * (step >> 2)) * PER, PER), 4 * PER)
                parts = [xr[b, rows, :] for b in range(windows)]
            else:
                rows = pl.ds(pl.multiple_of((first - off) * PER, PER), 4 * PER)
                parts = [rv[v - 1, b, rows, :] for b in range(windows)]
            beside(i)
            return dot(jnp.concatenate([half[i] for half in halves], axis=1), jnp.concatenate(parts, axis=0))

        p = [product(i) for i in range(9)]
        w0, w1 = p[0] + p[3], p[0] + p[6]
        for at, value in enumerate((w0 + (p[1] + p[4]), w0 + (p[2] + p[5]), w1 + (p[1] + p[7]), w1 + (p[2] + p[8]))):
            out_ref[0, at, 0] = (scale * value).astype(BF16)

    @pl.when(step < 4)
    def _():
        def beside(i):
            for n in range(i, 5 * windows, 9):
                make(jnp.maximum(18 - 5 * step - n // windows, 0), rv1, 0, (0, 1), (n % windows,))

        products(rv0, beside)

    @pl.when(step >= 4)
    def _():
        products(rv1, lambda i: None)


def flip(array, axis, by):
    return lax.ppermute(array, axis, [(i, i ^ by) for i in range(lax.axis_size(axis))])


def after(array, *others):
    return lax.optimization_barrier((array, *others))[0]


def block_shards(series, ref_list):
    chan_rows, time_len = series.shape
    groups, refs = ref_list.shape
    n_tm = lax.axis_size("tm")
    total = time_len * n_tm
    lags_dev = LAGS // n_tm
    group = lax.axis_index("chan").astype(jnp.int32)
    me = lax.axis_index("tm").astype(jnp.int32)
    smem = pl.BlockSpec(memory_space=pltpu.SMEM)
    vmem = pl.BlockSpec(memory_space=pltpu.VMEM)
    hbm = pl.BlockSpec(memory_space=pltpu.HBM)
    anywhere = pl.BlockSpec(memory_space=pl.ANY)
    own_pool, pair = pl.pallas_call(
        select_kernel,
        in_specs=[smem, vmem, hbm],
        out_specs=[vmem, vmem],
        out_shape=[jax.ShapeDtypeStruct((rows, time_len), BF16) for rows in (POOL, 2 * POOL)],
        scratch_shapes=[
            pltpu.VMEM((chan_rows, time_len), BF16),
            pltpu.VMEM((groups * chan_rows // 128, 128), F32),
            pltpu.SemaphoreType.DMA(()),
        ],
    )(group[None], ref_list, series)
    pool_x = flip(own_pool, "tm", 2)
    order = pl.pallas_call(
        functools.partial(order_kernel, per=chan_rows // 128),
        in_specs=[smem, vmem, hbm],
        out_specs=vmem,
        out_shape=jax.ShapeDtypeStruct((groups * POOL, refs), BF16),
        cost_estimate=pl.CostEstimate(flops=10**9, bytes_accessed=10**6, transcendentals=0),
    )(group[None], ref_list, own_pool)
    pair = lax.dynamic_update_slice(after(pair, order), pool_x, (POOL, 0))
    series_x = flip(after(series, pool_x, order), "tm", 2)
    along_z = [pair] + [flip(pair, "chan", 2 * d) for d in range(1, groups // 2)]
    pool = []
    for piece in along_z:
        pool += [piece, flip(piece, "chan", 1)]
    series_c = flip(after(series, *pool), "tm", 1)

    def phases(mine, other):
        return pl.pallas_call(
            series_kernel,
            in_specs=[smem, hbm, hbm],
            out_specs=vmem,
            out_shape=jax.ShapeDtypeStruct((9, chan_rows, time_len // 2), BF16),
            scratch_shapes=[pltpu.VMEM((chan_rows, 2 * time_len), BF16), pltpu.SemaphoreType.DMA((2,))],
            compiler_params=pltpu.CompilerParams(vmem_limit_bytes=16 * 2**20),
            cost_estimate=pl.CostEstimate(
                flops=1000, bytes_accessed=1000, transcendentals=0
            ),
        )((me & 1)[None], mine, other)

    first_half = phases(series, series_c)
    series_xc = flip(after(series_x, *pool), "tm", 1)
    halves = [first_half, phases(series_x, series_xc)]
    placed = pl.pallas_call(
        refs_kernel,
        in_specs=[vmem] * (1 + len(pool)),
        out_specs=vmem,
        out_shape=jax.ShapeDtypeStruct((2, PH, time_len // PH, refs), BF16),
        cost_estimate=pl.CostEstimate(flops=8 * 10**8, bytes_accessed=10**6, transcendentals=0),
    )(order, *pool)
    placed_c = flip(placed, "tm", 1)
    windows = total // WIN
    out = pl.pallas_call(
        functools.partial(corr_kernel, windows=windows, scale=1.0 / math.sqrt(total)),
        grid=(8,),
        in_specs=[smem] + [vmem] * 4,
        out_specs=pl.BlockSpec((1, 4, 1, chan_rows, refs), lambda i: (i // 4, 0, i % 4, 0, 0)),
        out_shape=jax.ShapeDtypeStruct((2, 4, 4, chan_rows, refs), BF16),
        scratch_shapes=[
            pltpu.VMEM((2, PH, total // PH + 8, 128), F32),
            pltpu.VMEM((windows, 47 * PER, refs), BF16),
            pltpu.VMEM((3, windows, 19 * PER, refs), BF16),
            pltpu.VMEM((3, windows, 19 * PER, refs), BF16),
        ],
        compiler_params=pltpu.CompilerParams(vmem_limit_bytes=40 * 2**20),
        cost_estimate=pl.CostEstimate(flops=15 * 10**9, bytes_accessed=2 * 10**7, transcendentals=0),
    )(me[None], placed, placed_c, *halves)
    return out.reshape(lags_dev, chan_rows, refs)


def solution(mesh):
    in_specs = (P("chan", "tm"), P())
    out_specs = P("tm", "chan", None)
    sizes = (mesh.shape["chan"], mesh.shape["tm"])
    body = block_shards if sizes == (8, 4) else general_shards
    return jax.shard_map(body, mesh=mesh, in_specs=in_specs, out_specs=out_specs, check_vma=False)
```

```python
import functools
import math

import jax
import jax.numpy as jnp
from jax import lax
from jax.experimental import pallas as pl
from jax.experimental.pallas import tpu as pltpu
from jax.sharding import PartitionSpec as P

LAGS = 128
POOL = 32
BF16 = jnp.bfloat16
F32 = jnp.float32


def dot(a, b):
    return jnp.dot(a, b, preferred_element_type=F32)


def shifted(array, axis, by):
    size = lax.axis_size(axis)
    pairs = [(i, i + by) for i in range(size) if 0 <= i + by < size]
    return lax.ppermute(array, axis, pairs)


def lag_block(extended_rows, ref_block, first_lag, time_len, scale_factor):
    offsets = first_lag + jnp.arange(8, dtype=jnp.int32)
    windows = jax.vmap(lambda offset: lax.dynamic_slice_in_dim(extended_rows, offset, time_len, 1))(
        offsets
    )
    return (
        jnp.einsum("jct,rt->jcr", windows, ref_block, preferred_element_type=jnp.float32)
        * scale_factor
    )


def general_shards(series, ref_list):
    chan_rows, time_len = series.shape
    ref_count = ref_list.shape[1]
    group_index = lax.axis_index("chan")
    my_list = lax.dynamic_index_in_dim(ref_list, group_index, 0, keepdims=False)
    gathered_all = lax.all_gather(series, "chan", axis=0, tiled=True)
    ref_rows = jnp.take(gathered_all, my_list, axis=0)
    lag_tail = shifted(series[:, :LAGS], "tm", -1)
    extended = jnp.concatenate([series, lag_tail], axis=1)
    scale_factor = 1.0 / math.sqrt(time_len * lax.axis_size("tm"))
    lags_dev = LAGS // lax.axis_size("tm")

    def lag_step(carry, block_index):
        return (carry, lag_block(extended, ref_rows, 8 * block_index, time_len, scale_factor))

    _, stacked = lax.scan(
        lag_step, None, jnp.arange(lax.axis_size("tm") * lags_dev // 8, dtype=jnp.int32)
    )
    return lax.psum_scatter(
        stacked.reshape(lax.axis_size("tm") * lags_dev, chan_rows, ref_count).astype(jnp.bfloat16),
        "tm",
        scatter_dimension=0,
        tiled=True,
    )


def ones_where(condition):
    return jnp.where(condition, 1.0, 0.0).astype(BF16)


def iota(shape, dim):
    return lax.broadcasted_iota(jnp.int32, shape, dim)


def nt_dot(a, b):
    return lax.dot_general(a, b, (((1,), (1,)), ((), ())), preferred_element_type=F32)


def marks_of(list_ref, highs):
    groups, width = list_ref.shape
    rows = [list_ref[g : g + 1, c : c + 128] for g in range(groups) for c in range(0, width, 128)]
    high = jnp.concatenate([ones_where(iota((highs, 128), 0) == (row >> 7)) for row in rows], axis=1)
    low = jnp.concatenate([ones_where(iota((128, 128), 0) == (row & 127)) for row in rows], axis=1)
    return high, low


def select_kernel(group_ref, list_hbm, s_hbm, pool_ref, pair_ref, list_ref, s_ref, rank_ref, sem):
    list_copy = pltpu.make_async_copy(list_hbm, list_ref, sem.at[0])
    list_copy.start()
    copy = pltpu.make_async_copy(s_hbm, s_ref, sem.at[1])
    copy.start()
    list_copy.wait()
    per = s_ref.shape[0] // 128
    highs = list_ref.shape[0] * per
    high, low = marks_of(list_ref, highs)
    named = nt_dot(high, low) > 0.5
    marks = ones_where(named)
    before = ones_where(iota((128, 128), 0) < iota((128, 128), 1))
    held = dot(marks, jnp.ones((128, 128), BF16)).astype(BF16)
    h_to, h_from = iota((highs, highs), 0), iota((highs, highs), 1)
    earlier = ones_where((h_to // per == h_from // per) & (h_from < h_to))
    rank_ref[...] = jnp.where(named, dot(marks, before) + dot(earlier, held), -1.0)
    slot = iota((POOL, 128), 0).astype(F32)
    picks = [
        ones_where(jnp.broadcast_to(rank_ref[pl.ds(group_ref[0] * per + h, 1), :], (POOL, 128)) == slot)
        for h in range(per)
    ]
    copy.wait()
    rows = dot(jnp.concatenate(picks, axis=1), s_ref[...]).astype(BF16)
    pool_ref[...] = rows
    pair_ref[:POOL] = rows
    pair_ref[POOL:] = jnp.zeros_like(rows)


def order_kernel(group_ref, list_ref, order_ref, *, per):
    groups, width = list_ref.shape
    highs = groups * per
    own = group_ref[0]
    high, low = marks_of(list_ref, highs)
    marks = ones_where(nt_dot(low, high) > 0.5)
    after = ones_where(iota((128, 128), 1) < iota((128, 128), 0))
    held = dot(jnp.ones((128, 128), BF16), marks).astype(BF16)
    h_from, h_to = iota((highs, highs), 0), iota((highs, highs), 1)
    earlier = ones_where((h_to // per == h_from // per) & (h_from < h_to))
    rank = dot(after, marks) + dot(held, earlier)
    place = rank + (POOL * ((iota((128, highs), 1) // per) ^ own)).astype(F32)
    mine = list_ref[pl.ds(own, 1), :]
    mine_high = ones_where(iota((highs, width), 0) == (mine >> 7))
    mine_low = jnp.where(iota((128, width), 0) == (mine & 127), 1.0, 0.0)
    at = jnp.sum(dot(place.astype(BF16), mine_high) * mine_low, axis=0, keepdims=True)
    order_ref[...] = ones_where(iota(order_ref.shape, 0).astype(F32) == at)


PH = 16
WIN = 512
PER = WIN // PH
QUARTER = WIN // 4
COMBOS = ((0, 0), (1, 0), (1, 4), (2, 0), (3, 0), (3, 4), (2, 8), (3, 8), (3, 12))


def series_kernel(core_ref, mine_ref, other_ref, out_ref, raw, sem):
    time_len = mine_ref.shape[1]
    copies = [
        pltpu.make_async_copy(
            ref, raw.at[:, pl.ds(pl.multiple_of((core_ref[0] ^ e) * time_len, 128), time_len)], sem.at[e]
        )
        for e, ref in enumerate((mine_ref, other_ref))
    ]
    for copy in copies:
        copy.start()
    at, to = iota((WIN, WIN), 0), iota((WIN, WIN), 1)
    turn = ones_where(at == PH * (to & (PER - 1)) + to // PER)
    for copy in copies:
        copy.wait()
    for b in range(raw.shape[1] // WIN):
        turned = dot(raw[:, b * WIN : (b + 1) * WIN], turn)
        t = [turned[:, QUARTER * g : QUARTER * (g + 1)] for g in range(4)]
        u0, u1 = t[0] + t[2], t[1] + t[3]
        sums = (u0 + u1, u1, -u0, t[2] + t[3], t[3], -t[2], -(t[0] + t[1]), -t[1], t[0])
        for i, value in enumerate(sums):
            out_ref[i, :, b * QUARTER : (b + 1) * QUARTER] = value.astype(BF16)


def refs_kernel(order_ref, *refs):
    *pieces, out_ref = refs
    time_len = pieces[0].shape[1]
    at, to = iota((256, 256), 0), iota((256, 256), 1)
    turn = ones_where(to == PH * (at & 15) + (at >> 4))
    blocks = [(x, b) for x in range(2) for b in range(time_len // 256)]
    turned = []
    for x, b in blocks:
        block = [piece[POOL * x : POOL * (x + 1), 256 * b : 256 * (b + 1)] for piece in pieces]
        turned.append(nt_dot(turn, jnp.concatenate(block, axis=0)).astype(BF16))
    placed = dot(jnp.concatenate(turned, axis=0), order_ref[...]).astype(BF16)
    for i, (x, b) in enumerate(blocks):
        for p in range(PH):
            out_ref[x, p, 16 * b : 16 * (b + 1), :] = placed[256 * i + 16 * p : 256 * i + 16 * (p + 1)]


def corr_kernel(tm_ref, mine_ref, other_ref, *refs, windows, scale):
    halves = refs[:2]
    out_ref, xf, xr, rv0, rv1 = refs[2:]
    me = tm_ref[0]
    half_w = windows // 2
    step = pl.program_id(0)

    def slab(idx):
        return pl.ds(pl.multiple_of(idx * PER, PER), PER)

    def make(idx, rv, base, which, windows_of):
        for b in windows_of:
            x0, x4, x8, x12 = (xr[b, slab(idx + o), :] for o in (0, 4, 8, 12))
            f0 = x4 - x0
            if 0 in which:
                rv[0, b, slab(idx - base), :] = f0
            if 1 in which:
                rv[1, b, slab(idx - base), :] = x8 - x0
            rv[2, b, slab(idx - base), :] = (x12 - x8) - f0

    @pl.when(step == 0)
    def _():
        block_rows = mine_ref.shape[2]
        for h in range(2):
            lanes = slice(128 * h, 128 * h + 128)
            for p in range(PH):
                xf[h, p, 0:8, :] = jnp.zeros((8, 128), F32)
                for c, ref in enumerate((mine_ref, other_ref)):
                    for x in range(2):
                        row = pl.multiple_of(8 + block_rows * (me ^ (c + 2 * x)), 8)
                        xf[h, p, pl.ds(row, block_rows), :] = ref[x, p, :, lanes].astype(F32)

        @pl.loop(0, 47)
        def _(idx):
            k = idx - 31
            for b in range(windows):
                half = (me >> 1) ^ (b // half_w)
                row = 8 + PER * (half_w * half + b % half_w) + (k >> 4) - 2 * me
                for h in range(2):
                    xr[b, slab(idx), 128 * h : 128 * h + 128] = xf[h, k & 15, pl.ds(row, PER), :].astype(BF16)

        for low, high, which in ((24, 35, (0, 1)), (20, 24, (1,)), (16, 20, ())):

            @pl.loop(low, high)
            def _(idx):
                make(idx, rv0, 16, which, range(windows))

    def products(rv, beside):
        first = 15 - (step & 3)

        def product(i):
            v, off = COMBOS[i]
            if v == 0:
                rows = pl.ds(pl.multiple_of((first + 16 - 16 * (step >> 2)) * PER, PER), 4 * PER)
                parts = [xr[b, rows, :] for b in range(windows)]
            else:
                rows = pl.ds(pl.multiple_of((first - off) * PER, PER), 4 * PER)
                parts = [rv[v - 1, b, rows, :] for b in range(windows)]
            beside(i)
            return dot(jnp.concatenate([half[i] for half in halves], axis=1), jnp.concatenate(parts, axis=0))

        p = [product(i) for i in range(9)]
        w0, w1 = p[0] + p[3], p[0] + p[6]
        for at, value in enumerate((w0 + (p[1] + p[4]), w0 + (p[2] + p[5]), w1 + (p[1] + p[7]), w1 + (p[2] + p[8]))):
            out_ref[0, at, 0] = (scale * value).astype(BF16)

    @pl.when(step < 4)
    def _():
        def beside(i):
            for n in range(i, 5 * windows, 9):
                make(jnp.maximum(18 - 5 * step - n // windows, 0), rv1, 0, (0, 1), (n % windows,))

        products(rv0, beside)

    @pl.when(step >= 4)
    def _():
        products(rv1, lambda i: None)


def flip(array, axis, by):
    return lax.ppermute(array, axis, [(i, i ^ by) for i in range(lax.axis_size(axis))])


def after(array, *others):
    return lax.optimization_barrier((array, *others))[0]


def block_shards(series, ref_list):
    chan_rows, time_len = series.shape
    groups, refs = ref_list.shape
    n_tm = lax.axis_size("tm")
    total = time_len * n_tm
    lags_dev = LAGS // n_tm
    group = lax.axis_index("chan").astype(jnp.int32)
    me = lax.axis_index("tm").astype(jnp.int32)
    smem = pl.BlockSpec(memory_space=pltpu.SMEM)
    vmem = pl.BlockSpec(memory_space=pltpu.VMEM)
    hbm = pl.BlockSpec(memory_space=pltpu.HBM)
    anywhere = pl.BlockSpec(memory_space=pl.ANY)
    small = pltpu.CompilerParams(vmem_limit_bytes=12 * 2**20)
    own_pool, pair = pl.pallas_call(
        select_kernel,
        in_specs=[smem, hbm, hbm],
        out_specs=[vmem, vmem],
        out_shape=[jax.ShapeDtypeStruct((rows, time_len), BF16) for rows in (POOL, 2 * POOL)],
        scratch_shapes=[
            pltpu.VMEM((groups, refs), jnp.int32),
            pltpu.VMEM((chan_rows, time_len), BF16),
            pltpu.VMEM((groups * chan_rows // 128, 128), F32),
            pltpu.SemaphoreType.DMA((2,)),
        ],
        compiler_params=pltpu.CompilerParams(vmem_limit_bytes=60 * 2**20),
    )(group[None], ref_list, series)
    pool_x = flip(own_pool, "tm", 2)
    order = pl.pallas_call(
        functools.partial(order_kernel, per=chan_rows // 128),
        in_specs=[smem, vmem],
        out_specs=vmem,
        out_shape=jax.ShapeDtypeStruct((groups * POOL, refs), BF16),
        compiler_params=small,
        cost_estimate=pl.CostEstimate(flops=10**9, bytes_accessed=10**6, transcendentals=0),
    )(group[None], after(ref_list, own_pool))
    pair = lax.dynamic_update_slice(after(pair, order), pool_x, (POOL, 0))
    series_x = flip(after(series, pool_x, order), "tm", 2)
    along_z = [pair, flip(pair, "chan", 2), flip(pair, "chan", 4)]
    along_z.append(flip(along_z[2], "chan", 2))
    pool = []
    for piece in along_z:
        pool += [piece, flip(piece, "chan", 1)]
    series_c = flip(after(series, *pool), "tm", 1)

    def phases(mine, other):
        return pl.pallas_call(
            series_kernel,
            in_specs=[smem, hbm, hbm],
            out_specs=vmem,
            out_shape=jax.ShapeDtypeStruct((9, chan_rows, time_len // 2), BF16),
            scratch_shapes=[pltpu.VMEM((chan_rows, 2 * time_len), BF16), pltpu.SemaphoreType.DMA((2,))],
            compiler_params=pltpu.CompilerParams(vmem_limit_bytes=16 * 2**20),
            cost_estimate=pl.CostEstimate(
                flops=1000, bytes_accessed=1000, transcendentals=0
            ),
        )((me & 1)[None], mine, other)

    first_half = phases(series, series_c)
    series_xc = flip(after(series_x, *pool), "tm", 1)
    halves = [first_half, phases(series_x, series_xc)]
    placed = pl.pallas_call(
        refs_kernel,
        in_specs=[vmem] * (1 + len(pool)),
        out_specs=vmem,
        out_shape=jax.ShapeDtypeStruct((2, PH, time_len // PH, refs), BF16),
        compiler_params=small,
        cost_estimate=pl.CostEstimate(flops=8 * 10**8, bytes_accessed=10**6, transcendentals=0),
    )(order, *pool)
    placed_c = flip(placed, "tm", 1)
    windows = total // WIN
    out = pl.pallas_call(
        functools.partial(corr_kernel, windows=windows, scale=1.0 / math.sqrt(total)),
        grid=(8,),
        in_specs=[smem] + [vmem] * 4,
        out_specs=pl.BlockSpec((1, 4, 1, chan_rows, refs), lambda i: (i // 4, 0, i % 4, 0, 0)),
        out_shape=jax.ShapeDtypeStruct((2, 4, 4, chan_rows, refs), BF16),
        scratch_shapes=[
            pltpu.VMEM((2, PH, total // PH + 8, 128), F32),
            pltpu.VMEM((windows, 47 * PER, refs), BF16),
            pltpu.VMEM((3, windows, 19 * PER, refs), BF16),
            pltpu.VMEM((3, windows, 19 * PER, refs), BF16),
        ],
        compiler_params=pltpu.CompilerParams(vmem_limit_bytes=40 * 2**20),
        cost_estimate=pl.CostEstimate(flops=15 * 10**9, bytes_accessed=2 * 10**7, transcendentals=0),
    )(me[None], placed, placed_c, *halves)
    return out.reshape(lags_dev, chan_rows, refs)


def solution(mesh):
    in_specs = (P("chan", "tm"), P())
    out_specs = P("tm", "chan", None)
    sizes = (mesh.shape["chan"], mesh.shape["tm"])
    body = block_shards if sizes == (8, 4) else general_shards
    return jax.shard_map(body, mesh=mesh, in_specs=in_specs, out_specs=out_specs, check_vma=False)
```

```python
import functools
import math

import jax
import jax.numpy as jnp
from jax import lax
from jax.experimental import pallas as pl
from jax.experimental.pallas import tpu as pltpu
from jax.sharding import PartitionSpec as P

LAGS = 128
POOL = 32
BF16 = jnp.bfloat16
F32 = jnp.float32


def dot(a, b):
    return jnp.dot(a, b, preferred_element_type=F32)


def shifted(array, axis, by):
    size = lax.axis_size(axis)
    pairs = [(i, i + by) for i in range(size) if 0 <= i + by < size]
    return lax.ppermute(array, axis, pairs)


def lag_block(extended_rows, ref_block, first_lag, time_len, scale_factor):
    offsets = first_lag + jnp.arange(8, dtype=jnp.int32)
    windows = jax.vmap(lambda offset: lax.dynamic_slice_in_dim(extended_rows, offset, time_len, 1))(
        offsets
    )
    return (
        jnp.einsum("jct,rt->jcr", windows, ref_block, preferred_element_type=jnp.float32)
        * scale_factor
    )


def general_shards(series, ref_list):
    chan_rows, time_len = series.shape
    ref_count = ref_list.shape[1]
    group_index = lax.axis_index("chan")
    my_list = lax.dynamic_index_in_dim(ref_list, group_index, 0, keepdims=False)
    gathered_all = lax.all_gather(series, "chan", axis=0, tiled=True)
    ref_rows = jnp.take(gathered_all, my_list, axis=0)
    lag_tail = shifted(series[:, :LAGS], "tm", -1)
    extended = jnp.concatenate([series, lag_tail], axis=1)
    scale_factor = 1.0 / math.sqrt(time_len * lax.axis_size("tm"))
    lags_dev = LAGS // lax.axis_size("tm")

    def lag_step(carry, block_index):
        return (carry, lag_block(extended, ref_rows, 8 * block_index, time_len, scale_factor))

    _, stacked = lax.scan(
        lag_step, None, jnp.arange(lax.axis_size("tm") * lags_dev // 8, dtype=jnp.int32)
    )
    return lax.psum_scatter(
        stacked.reshape(lax.axis_size("tm") * lags_dev, chan_rows, ref_count).astype(jnp.bfloat16),
        "tm",
        scatter_dimension=0,
        tiled=True,
    )


def ones_where(condition):
    return jnp.where(condition, 1.0, 0.0).astype(BF16)


def iota(shape, dim):
    return lax.broadcasted_iota(jnp.int32, shape, dim)


def nt_dot(a, b):
    return lax.dot_general(a, b, (((1,), (1,)), ((), ())), preferred_element_type=F32)


def marks_of(list_ref, highs):
    groups, width = list_ref.shape
    rows = [list_ref[g : g + 1, c : c + 128] for g in range(groups) for c in range(0, width, 128)]
    high = jnp.concatenate([ones_where(iota((highs, 128), 0) == (row >> 7)) for row in rows], axis=1)
    low = jnp.concatenate([ones_where(iota((128, 128), 0) == (row & 127)) for row in rows], axis=1)
    return high, low


def select_kernel(group_ref, list_hbm, s_hbm, pool_ref, pair_ref, list_ref, s_ref, rank_ref, sem):
    list_copy = pltpu.make_async_copy(list_hbm, list_ref, sem.at[0])
    list_copy.start()
    copy = pltpu.make_async_copy(s_hbm, s_ref, sem.at[1])
    copy.start()
    list_copy.wait()
    per = s_ref.shape[0] // 128
    highs = list_ref.shape[0] * per
    high, low = marks_of(list_ref, highs)
    named = nt_dot(high, low) > 0.5
    marks = ones_where(named)
    before = ones_where(iota((128, 128), 0) < iota((128, 128), 1))
    held = dot(marks, jnp.ones((128, 128), BF16)).astype(BF16)
    h_to, h_from = iota((highs, highs), 0), iota((highs, highs), 1)
    earlier = ones_where((h_to // per == h_from // per) & (h_from < h_to))
    rank_ref[...] = jnp.where(named, dot(marks, before) + dot(earlier, held), -1.0)
    slot = iota((POOL, 128), 0).astype(F32)
    picks = [
        ones_where(jnp.broadcast_to(rank_ref[pl.ds(group_ref[0] * per + h, 1), :], (POOL, 128)) == slot)
        for h in range(per)
    ]
    copy.wait()
    rows = dot(jnp.concatenate(picks, axis=1), s_ref[...]).astype(BF16)
    pool_ref[...] = rows
    pair_ref[:POOL] = rows
    pair_ref[POOL:] = jnp.zeros_like(rows)


def order_kernel(group_ref, list_ref, order_ref, *, per):
    groups, width = list_ref.shape
    highs = groups * per
    own = group_ref[0]
    high, low = marks_of(list_ref, highs)
    marks = ones_where(nt_dot(low, high) > 0.5)
    after = ones_where(iota((128, 128), 1) < iota((128, 128), 0))
    held = dot(jnp.ones((128, 128), BF16), marks).astype(BF16)
    h_from, h_to = iota((highs, highs), 0), iota((highs, highs), 1)
    earlier = ones_where((h_to // per == h_from // per) & (h_from < h_to))
    rank = dot(after, marks) + dot(held, earlier)
    place = rank + (POOL * ((iota((128, highs), 1) // per) ^ own)).astype(F32)
    mine = list_ref[pl.ds(own, 1), :]
    mine_high = ones_where(iota((highs, width), 0) == (mine >> 7))
    mine_low = jnp.where(iota((128, width), 0) == (mine & 127), 1.0, 0.0)
    at = jnp.sum(dot(place.astype(BF16), mine_high) * mine_low, axis=0, keepdims=True)
    order_ref[...] = ones_where(iota(order_ref.shape, 0).astype(F32) == at)


PH = 16
WIN = 512
PER = WIN // PH
QUARTER = WIN // 4
COMBOS = ((0, 0), (1, 0), (1, 4), (2, 0), (3, 0), (3, 4), (2, 8), (3, 8), (3, 12))


def series_kernel(core_ref, mine_ref, other_ref, out_ref, raw, sem):
    time_len = mine_ref.shape[1]
    copies = [
        pltpu.make_async_copy(
            ref, raw.at[:, pl.ds(pl.multiple_of((core_ref[0] ^ e) * time_len, 128), time_len)], sem.at[e]
        )
        for e, ref in enumerate((mine_ref, other_ref))
    ]
    for copy in copies:
        copy.start()
    at, to = iota((WIN, WIN), 0), iota((WIN, WIN), 1)
    turn = ones_where(at == PH * (to & (PER - 1)) + to // PER)
    for copy in copies:
        copy.wait()
    for b in range(raw.shape[1] // WIN):
        turned = dot(raw[:, b * WIN : (b + 1) * WIN], turn)
        t = [turned[:, QUARTER * g : QUARTER * (g + 1)] for g in range(4)]
        u0, u1 = t[0] + t[2], t[1] + t[3]
        sums = (u0 + u1, u1, -u0, t[2] + t[3], t[3], -t[2], -(t[0] + t[1]), -t[1], t[0])
        for i, value in enumerate(sums):
            out_ref[i, :, b * QUARTER : (b + 1) * QUARTER] = value.astype(BF16)


def refs_kernel(order_ref, *refs):
    *pieces, out_ref = refs
    time_len = pieces[0].shape[1]
    at, to = iota((256, 256), 0), iota((256, 256), 1)
    turn = ones_where(to == PH * (at & 15) + (at >> 4))
    blocks = [(x, b) for x in range(2) for b in range(time_len // 256)]
    turned = []
    for x, b in blocks:
        block = [piece[POOL * x : POOL * (x + 1), 256 * b : 256 * (b + 1)] for piece in pieces]
        turned.append(nt_dot(turn, jnp.concatenate(block, axis=0)).astype(BF16))
    placed = dot(jnp.concatenate(turned, axis=0), order_ref[...]).astype(BF16)
    for i, (x, b) in enumerate(blocks):
        for p in range(PH):
            out_ref[x, p, 16 * b : 16 * (b + 1), :] = placed[256 * i + 16 * p : 256 * i + 16 * (p + 1)]


def corr_kernel(tm_ref, mine_ref, other_ref, *refs, windows, scale):
    halves = refs[:2]
    out_ref, xf, xr, rv0, rv1 = refs[2:]
    me = tm_ref[0]
    half_w = windows // 2
    step = pl.program_id(0)

    def slab(idx):
        return pl.ds(pl.multiple_of(idx * PER, PER), PER)

    def make(idx, rv, base, which, windows_of):
        for b in windows_of:
            x0, x4, x8, x12 = (xr[b, slab(idx + o), :] for o in (0, 4, 8, 12))
            f0 = x4 - x0
            if 0 in which:
                rv[0, b, slab(idx - base), :] = f0
            if 1 in which:
                rv[1, b, slab(idx - base), :] = x8 - x0
            rv[2, b, slab(idx - base), :] = (x12 - x8) - f0

    @pl.when(step == 0)
    def _():
        block_rows = mine_ref.shape[2]
        for h in range(2):
            lanes = slice(128 * h, 128 * h + 128)
            for p in range(PH):
                xf[h, p, 0:8, :] = jnp.zeros((8, 128), F32)
                for c, ref in enumerate((mine_ref, other_ref)):
                    for x in range(2):
                        row = pl.multiple_of(8 + block_rows * (me ^ (c + 2 * x)), 8)
                        xf[h, p, pl.ds(row, block_rows), :] = ref[x, p, :, lanes].astype(F32)

        @pl.loop(0, 47)
        def _(idx):
            k = idx - 31
            for b in range(windows):
                half = (me >> 1) ^ (b // half_w)
                row = 8 + PER * (half_w * half + b % half_w) + (k >> 4) - 2 * me
                for h in range(2):
                    xr[b, slab(idx), 128 * h : 128 * h + 128] = xf[h, k & 15, pl.ds(row, PER), :].astype(BF16)

        for low, high, which in ((24, 35, (0, 1)), (20, 24, (1,)), (16, 20, ())):

            @pl.loop(low, high)
            def _(idx):
                make(idx, rv0, 16, which, range(windows))

    def products(rv, beside):
        first = 15 - (step & 3)

        def product(i):
            v, off = COMBOS[i]
            if v == 0:
                rows = pl.ds(pl.multiple_of((first + 16 - 16 * (step >> 2)) * PER, PER), 4 * PER)
                parts = [xr[b, rows, :] for b in range(windows)]
            else:
                rows = pl.ds(pl.multiple_of((first - off) * PER, PER), 4 * PER)
                parts = [rv[v - 1, b, rows, :] for b in range(windows)]
            beside(i)
            return dot(jnp.concatenate([half[i] for half in halves], axis=1), jnp.concatenate(parts, axis=0))

        p = [product(i) for i in range(9)]
        w0, w1 = p[0] + p[3], p[0] + p[6]
        for at, value in enumerate((w0 + (p[1] + p[4]), w0 + (p[2] + p[5]), w1 + (p[1] + p[7]), w1 + (p[2] + p[8]))):
            out_ref[0, at, 0] = (scale * value).astype(BF16)

    @pl.when(step < 4)
    def _():
        def beside(i):
            for n in range(i, 5 * windows, 9):
                make(jnp.maximum(18 - 5 * step - n // windows, 0), rv1, 0, (0, 1), (n % windows,))

        products(rv0, beside)

    @pl.when(step >= 4)
    def _():
        products(rv1, lambda i: None)


def flip(array, axis, by):
    return lax.ppermute(array, axis, [(i, i ^ by) for i in range(lax.axis_size(axis))])


def after(array, *others):
    return lax.optimization_barrier((array, *others))[0]


def block_shards(series, ref_list):
    chan_rows, time_len = series.shape
    groups, refs = ref_list.shape
    n_tm = lax.axis_size("tm")
    total = time_len * n_tm
    lags_dev = LAGS // n_tm
    group = lax.axis_index("chan").astype(jnp.int32)
    me = lax.axis_index("tm").astype(jnp.int32)
    smem = pl.BlockSpec(memory_space=pltpu.SMEM)
    vmem = pl.BlockSpec(memory_space=pltpu.VMEM)
    hbm = pl.BlockSpec(memory_space=pltpu.HBM)
    anywhere = pl.BlockSpec(memory_space=pl.ANY)
    small = pltpu.CompilerParams(vmem_limit_bytes=12 * 2**20)
    own_pool, pair = pl.pallas_call(
        select_kernel,
        in_specs=[smem, hbm, hbm],
        out_specs=[vmem, vmem],
        out_shape=[jax.ShapeDtypeStruct((rows, time_len), BF16) for rows in (POOL, 2 * POOL)],
        scratch_shapes=[
            pltpu.VMEM((groups, refs), jnp.int32),
            pltpu.VMEM((chan_rows, time_len), BF16),
            pltpu.VMEM((groups * chan_rows // 128, 128), F32),
            pltpu.SemaphoreType.DMA((2,)),
        ],
        compiler_params=pltpu.CompilerParams(vmem_limit_bytes=60 * 2**20),
    )(group[None], ref_list, series)
    pool_x = flip(own_pool, "tm", 2)
    order = pl.pallas_call(
        functools.partial(order_kernel, per=chan_rows // 128),
        in_specs=[smem, vmem],
        out_specs=vmem,
        out_shape=jax.ShapeDtypeStruct((groups * POOL, refs), BF16),
        compiler_params=small,
        cost_estimate=pl.CostEstimate(flops=10**9, bytes_accessed=10**6, transcendentals=0),
    )(group[None], after(ref_list, own_pool))
    series_c = flip(after(series, own_pool), "tm", 1)
    pair = lax.dynamic_update_slice(after(pair, order, series_c), pool_x, (POOL, 0))
    series_x = flip(after(series, pool_x, order), "tm", 2)
    along_z = [pair, flip(pair, "chan", 2), flip(pair, "chan", 4)]
    along_z.append(flip(along_z[2], "chan", 2))
    pool = []
    for piece in along_z:
        pool += [piece, flip(piece, "chan", 1)]

    def phases(mine, other):
        return pl.pallas_call(
            series_kernel,
            in_specs=[smem, hbm, hbm],
            out_specs=vmem,
            out_shape=jax.ShapeDtypeStruct((9, chan_rows, time_len // 2), BF16),
            scratch_shapes=[pltpu.VMEM((chan_rows, 2 * time_len), BF16), pltpu.SemaphoreType.DMA((2,))],
            compiler_params=pltpu.CompilerParams(vmem_limit_bytes=16 * 2**20),
            cost_estimate=pl.CostEstimate(
                flops=1000, bytes_accessed=1000, transcendentals=0
            ),
        )((me & 1)[None], mine, other)

    first_half = phases(series, series_c)
    series_xc = flip(after(series_x, *pool), "tm", 1)
    halves = [first_half, phases(series_x, series_xc)]
    placed = pl.pallas_call(
        refs_kernel,
        in_specs=[vmem] * (1 + len(pool)),
        out_specs=vmem,
        out_shape=jax.ShapeDtypeStruct((2, PH, time_len // PH, refs), BF16),
        compiler_params=small,
        cost_estimate=pl.CostEstimate(flops=8 * 10**8, bytes_accessed=10**6, transcendentals=0),
    )(after(order, halves[0]), *pool)
    placed_c = flip(placed, "tm", 1)
    windows = total // WIN
    out = pl.pallas_call(
        functools.partial(corr_kernel, windows=windows, scale=1.0 / math.sqrt(total)),
        grid=(8,),
        in_specs=[smem] + [vmem] * 4,
        out_specs=pl.BlockSpec((1, 4, 1, chan_rows, refs), lambda i: (i // 4, 0, i % 4, 0, 0)),
        out_shape=jax.ShapeDtypeStruct((2, 4, 4, chan_rows, refs), BF16),
        scratch_shapes=[
            pltpu.VMEM((2, PH, total // PH + 8, 128), F32),
            pltpu.VMEM((windows, 47 * PER, refs), BF16),
            pltpu.VMEM((3, windows, 19 * PER, refs), BF16),
            pltpu.VMEM((3, windows, 19 * PER, refs), BF16),
        ],
        compiler_params=pltpu.CompilerParams(vmem_limit_bytes=40 * 2**20),
        cost_estimate=pl.CostEstimate(flops=15 * 10**9, bytes_accessed=2 * 10**7, transcendentals=0),
    )(me[None], placed, placed_c, *halves)
    return out.reshape(lags_dev, chan_rows, refs)


def solution(mesh):
    in_specs = (P("chan", "tm"), P())
    out_specs = P("tm", "chan", None)
    sizes = (mesh.shape["chan"], mesh.shape["tm"])
    body = block_shards if sizes == (8, 4) else general_shards
    return jax.shard_map(body, mesh=mesh, in_specs=in_specs, out_specs=out_specs, check_vma=False)
```

```python
import functools
import math

import jax
import jax.numpy as jnp
from jax import lax
from jax.experimental import pallas as pl
from jax.experimental.pallas import tpu as pltpu
from jax.sharding import PartitionSpec as P

LAGS = 128
POOL = 32
BF16 = jnp.bfloat16
F32 = jnp.float32


def dot(a, b):
    return jnp.dot(a, b, preferred_element_type=F32)


def shifted(array, axis, by):
    size = lax.axis_size(axis)
    pairs = [(i, i + by) for i in range(size) if 0 <= i + by < size]
    return lax.ppermute(array, axis, pairs)


def lag_block(extended_rows, ref_block, first_lag, time_len, scale_factor):
    offsets = first_lag + jnp.arange(8, dtype=jnp.int32)
    windows = jax.vmap(lambda offset: lax.dynamic_slice_in_dim(extended_rows, offset, time_len, 1))(
        offsets
    )
    return (
        jnp.einsum("jct,rt->jcr", windows, ref_block, preferred_element_type=jnp.float32)
        * scale_factor
    )


def general_shards(series, ref_list):
    chan_rows, time_len = series.shape
    ref_count = ref_list.shape[1]
    group_index = lax.axis_index("chan")
    my_list = lax.dynamic_index_in_dim(ref_list, group_index, 0, keepdims=False)
    gathered_all = lax.all_gather(series, "chan", axis=0, tiled=True)
    ref_rows = jnp.take(gathered_all, my_list, axis=0)
    lag_tail = shifted(series[:, :LAGS], "tm", -1)
    extended = jnp.concatenate([series, lag_tail], axis=1)
    scale_factor = 1.0 / math.sqrt(time_len * lax.axis_size("tm"))
    lags_dev = LAGS // lax.axis_size("tm")

    def lag_step(carry, block_index):
        return (carry, lag_block(extended, ref_rows, 8 * block_index, time_len, scale_factor))

    _, stacked = lax.scan(
        lag_step, None, jnp.arange(lax.axis_size("tm") * lags_dev // 8, dtype=jnp.int32)
    )
    return lax.psum_scatter(
        stacked.reshape(lax.axis_size("tm") * lags_dev, chan_rows, ref_count).astype(jnp.bfloat16),
        "tm",
        scatter_dimension=0,
        tiled=True,
    )


def ones_where(condition):
    return jnp.where(condition, 1.0, 0.0).astype(BF16)


def iota(shape, dim):
    return lax.broadcasted_iota(jnp.int32, shape, dim)


def nt_dot(a, b):
    return lax.dot_general(a, b, (((1,), (1,)), ((), ())), preferred_element_type=F32)


def marks_of(list_ref, highs):
    groups, width = list_ref.shape
    rows = [list_ref[g : g + 1, c : c + 128] for g in range(groups) for c in range(0, width, 128)]
    high = jnp.concatenate([ones_where(iota((highs, 128), 0) == (row >> 7)) for row in rows], axis=1)
    low = jnp.concatenate([ones_where(iota((128, 128), 0) == (row & 127)) for row in rows], axis=1)
    return high, low


def select_kernel(group_ref, list_hbm, s_hbm, pool_ref, pair_ref, list_ref, s_ref, rank_ref, sem):
    list_copy = pltpu.make_async_copy(list_hbm, list_ref, sem.at[0])
    list_copy.start()
    copy = pltpu.make_async_copy(s_hbm, s_ref, sem.at[1])
    copy.start()
    list_copy.wait()
    per = s_ref.shape[0] // 128
    highs = list_ref.shape[0] * per
    high, low = marks_of(list_ref, highs)
    named = nt_dot(high, low) > 0.5
    marks = ones_where(named)
    before = ones_where(iota((128, 128), 0) < iota((128, 128), 1))
    held = dot(marks, jnp.ones((128, 128), BF16)).astype(BF16)
    h_to, h_from = iota((highs, highs), 0), iota((highs, highs), 1)
    earlier = ones_where((h_to // per == h_from // per) & (h_from < h_to))
    rank_ref[...] = jnp.where(named, dot(marks, before) + dot(earlier, held), -1.0)
    slot = iota((POOL, 128), 0).astype(F32)
    picks = [
        ones_where(jnp.broadcast_to(rank_ref[pl.ds(group_ref[0] * per + h, 1), :], (POOL, 128)) == slot)
        for h in range(per)
    ]
    copy.wait()
    rows = dot(jnp.concatenate(picks, axis=1), s_ref[...]).astype(BF16)
    pool_ref[...] = rows
    pair_ref[:POOL] = rows
    pair_ref[POOL:] = jnp.zeros_like(rows)


def order_kernel(group_ref, list_ref, order_ref, *, per):
    groups, width = list_ref.shape
    highs = groups * per
    own = group_ref[0]
    high, low = marks_of(list_ref, highs)
    marks = ones_where(nt_dot(low, high) > 0.5)
    after = ones_where(iota((128, 128), 1) < iota((128, 128), 0))
    held = dot(jnp.ones((128, 128), BF16), marks).astype(BF16)
    h_from, h_to = iota((highs, highs), 0), iota((highs, highs), 1)
    earlier = ones_where((h_to // per == h_from // per) & (h_from < h_to))
    rank = dot(after, marks) + dot(held, earlier)
    place = rank + (POOL * ((iota((128, highs), 1) // per) ^ own)).astype(F32)
    mine = list_ref[pl.ds(own, 1), :]
    mine_high = ones_where(iota((highs, width), 0) == (mine >> 7))
    mine_low = jnp.where(iota((128, width), 0) == (mine & 127), 1.0, 0.0)
    at = jnp.sum(dot(place.astype(BF16), mine_high) * mine_low, axis=0, keepdims=True)
    order_ref[...] = ones_where(iota(order_ref.shape, 0).astype(F32) == at)


PH = 16
WIN = 512
PER = WIN // PH
QUARTER = WIN // 4
COMBOS = ((0, 0), (1, 0), (1, 4), (2, 0), (3, 0), (3, 4), (2, 8), (3, 8), (3, 12))


def series_kernel(core_ref, mine_ref, other_ref, out_ref, raw, sem):
    time_len = mine_ref.shape[1]
    copies = [
        pltpu.make_async_copy(
            ref, raw.at[:, pl.ds(pl.multiple_of((core_ref[0] ^ e) * time_len, 128), time_len)], sem.at[e]
        )
        for e, ref in enumerate((mine_ref, other_ref))
    ]
    for copy in copies:
        copy.start()
    at, to = iota((WIN, WIN), 0), iota((WIN, WIN), 1)
    turn = ones_where(at == PH * (to & (PER - 1)) + to // PER)
    for copy in copies:
        copy.wait()
    for b in range(raw.shape[1] // WIN):
        turned = dot(raw[:, b * WIN : (b + 1) * WIN], turn)
        t = [turned[:, QUARTER * g : QUARTER * (g + 1)] for g in range(4)]
        u0, u1 = t[0] + t[2], t[1] + t[3]
        sums = (u0 + u1, u1, -u0, t[2] + t[3], t[3], -t[2], -(t[0] + t[1]), -t[1], t[0])
        for i, value in enumerate(sums):
            out_ref[i, :, b * QUARTER : (b + 1) * QUARTER] = value.astype(BF16)


def refs_kernel(order_ref, *refs):
    *pieces, out_ref = refs
    time_len = pieces[0].shape[1]
    at, to = iota((256, 256), 0), iota((256, 256), 1)
    turn = ones_where(to == PH * (at & 15) + (at >> 4))
    blocks = [(x, b) for x in range(2) for b in range(time_len // 256)]
    turned = []
    for x, b in blocks:
        block = [piece[POOL * x : POOL * (x + 1), 256 * b : 256 * (b + 1)] for piece in pieces]
        turned.append(nt_dot(turn, jnp.concatenate(block, axis=0)).astype(BF16))
    placed = dot(jnp.concatenate(turned, axis=0), order_ref[...]).astype(BF16)
    for i, (x, b) in enumerate(blocks):
        for p in range(PH):
            out_ref[x, p, 16 * b : 16 * (b + 1), :] = placed[256 * i + 16 * p : 256 * i + 16 * (p + 1)]


def slab(idx):
    return pl.ds(pl.multiple_of(idx * PER, PER), PER)


def make(xr, idx, rv, base, which, windows_of):
    for b in windows_of:
        x0, x4, x8, x12 = (xr[b, slab(idx + o), :] for o in (0, 4, 8, 12))
        f0 = x4 - x0
        if 0 in which:
            rv[0, b, slab(idx - base), :] = f0
        if 1 in which:
            rv[1, b, slab(idx - base), :] = x8 - x0
        rv[2, b, slab(idx - base), :] = (x12 - x8) - f0


def lag_kernel(tm_ref, mine_ref, other_ref, xr, rv0, xf):
    me = tm_ref[0]
    windows = xr.shape[0]
    half_w = windows // 2
    block_rows = mine_ref.shape[2]
    for h in range(2):
        lanes = slice(128 * h, 128 * h + 128)
        for p in range(PH):
            xf[h, p, 0:8, :] = jnp.zeros((8, 128), F32)
            for c, ref in enumerate((mine_ref, other_ref)):
                for x in range(2):
                    row = pl.multiple_of(8 + block_rows * (me ^ (c + 2 * x)), 8)
                    xf[h, p, pl.ds(row, block_rows), :] = ref[x, p, :, lanes].astype(F32)

    @pl.loop(0, 47)
    def _(idx):
        k = idx - 31
        for b in range(windows):
            half = (me >> 1) ^ (b // half_w)
            row = 8 + PER * (half_w * half + b % half_w) + (k >> 4) - 2 * me
            for h in range(2):
                xr[b, slab(idx), 128 * h : 128 * h + 128] = xf[h, k & 15, pl.ds(row, PER), :].astype(BF16)

    for low, high, which in ((24, 35, (0, 1)), (20, 24, (1,)), (16, 20, ())):

        @pl.loop(low, high)
        def _(idx):
            make(xr, idx, rv0, 16, which, range(windows))


def corr_kernel(xr, rv0, *refs, windows, scale):
    *halves, out_ref, rv1 = refs
    step = pl.program_id(0)

    def products(rv, beside):
        first = 15 - (step & 3)

        def product(i):
            v, off = COMBOS[i]
            if v == 0:
                rows = pl.ds(pl.multiple_of((first + 16 - 16 * (step >> 2)) * PER, PER), 4 * PER)
                parts = [xr[b, rows, :] for b in range(windows)]
            else:
                rows = pl.ds(pl.multiple_of((first - off) * PER, PER), 4 * PER)
                parts = [rv[v - 1, b, rows, :] for b in range(windows)]
            beside(i)
            return dot(jnp.concatenate([half[i] for half in halves], axis=1), jnp.concatenate(parts, axis=0))

        p = [product(i) for i in range(9)]
        w0, w1 = p[0] + p[3], p[0] + p[6]
        for at, value in enumerate((w0 + (p[1] + p[4]), w0 + (p[2] + p[5]), w1 + (p[1] + p[7]), w1 + (p[2] + p[8]))):
            out_ref[0, at, 0] = (scale * value).astype(BF16)

    @pl.when(step < 4)
    def _():
        def beside(i):
            for n in range(i, 5 * windows, 9):
                make(xr, jnp.maximum(18 - 5 * step - n // windows, 0), rv1, 0, (0, 1), (n % windows,))

        products(rv0, beside)

    @pl.when(step >= 4)
    def _():
        products(rv1, lambda i: None)


def flip(array, axis, by):
    return lax.ppermute(array, axis, [(i, i ^ by) for i in range(lax.axis_size(axis))])


def after(array, *others):
    return lax.optimization_barrier((array, *others))[0]


def block_shards(series, ref_list):
    chan_rows, time_len = series.shape
    groups, refs = ref_list.shape
    n_tm = lax.axis_size("tm")
    total = time_len * n_tm
    lags_dev = LAGS // n_tm
    group = lax.axis_index("chan").astype(jnp.int32)
    me = lax.axis_index("tm").astype(jnp.int32)
    smem = pl.BlockSpec(memory_space=pltpu.SMEM)
    vmem = pl.BlockSpec(memory_space=pltpu.VMEM)
    hbm = pl.BlockSpec(memory_space=pltpu.HBM)
    anywhere = pl.BlockSpec(memory_space=pl.ANY)
    small = pltpu.CompilerParams(vmem_limit_bytes=12 * 2**20)
    own_pool, pair = pl.pallas_call(
        select_kernel,
        in_specs=[smem, hbm, hbm],
        out_specs=[vmem, vmem],
        out_shape=[jax.ShapeDtypeStruct((rows, time_len), BF16) for rows in (POOL, 2 * POOL)],
        scratch_shapes=[
            pltpu.VMEM((groups, refs), jnp.int32),
            pltpu.VMEM((chan_rows, time_len), BF16),
            pltpu.VMEM((groups * chan_rows // 128, 128), F32),
            pltpu.SemaphoreType.DMA((2,)),
        ],
        compiler_params=pltpu.CompilerParams(vmem_limit_bytes=48 * 2**20),
    )(group[None], ref_list, series)
    pool_x = flip(own_pool, "tm", 2)
    order = pl.pallas_call(
        functools.partial(order_kernel, per=chan_rows // 128),
        in_specs=[smem, vmem],
        out_specs=vmem,
        out_shape=jax.ShapeDtypeStruct((groups * POOL, refs), BF16),
        compiler_params=small,
        cost_estimate=pl.CostEstimate(flops=10**9, bytes_accessed=10**6, transcendentals=0),
    )(group[None], after(ref_list, own_pool))
    series_c = flip(after(series, own_pool), "tm", 1)
    pair = lax.dynamic_update_slice(after(pair, order, series_c), pool_x, (POOL, 0))
    series_x = flip(after(series, pool_x, order), "tm", 2)
    along_z = [pair, flip(pair, "chan", 2), flip(pair, "chan", 4)]
    along_z.append(flip(along_z[2], "chan", 2))
    pool = []
    for piece in along_z:
        pool += [piece, flip(piece, "chan", 1)]

    def phases(mine, other):
        return pl.pallas_call(
            series_kernel,
            in_specs=[smem, hbm, hbm],
            out_specs=vmem,
            out_shape=jax.ShapeDtypeStruct((9, chan_rows, time_len // 2), BF16),
            scratch_shapes=[pltpu.VMEM((chan_rows, 2 * time_len), BF16), pltpu.SemaphoreType.DMA((2,))],
            compiler_params=pltpu.CompilerParams(vmem_limit_bytes=16 * 2**20),
            cost_estimate=pl.CostEstimate(
                flops=1000, bytes_accessed=1000, transcendentals=0
            ),
        )((me & 1)[None], mine, other)

    first_half = phases(series, series_c)
    placed = pl.pallas_call(
        refs_kernel,
        in_specs=[vmem] * (1 + len(pool)),
        out_specs=vmem,
        out_shape=jax.ShapeDtypeStruct((2, PH, time_len // PH, refs), BF16),
        compiler_params=small,
        cost_estimate=pl.CostEstimate(flops=8 * 10**8, bytes_accessed=10**6, transcendentals=0),
    )(after(order, first_half), *pool)
    placed_c = flip(placed, "tm", 1)
    series_xc = flip(after(series_x, placed), "tm", 1)
    windows = total // WIN
    shifted_refs, differences = pl.pallas_call(
        lag_kernel,
        in_specs=[smem, vmem, vmem],
        out_specs=[vmem] * 2,
        out_shape=[
            jax.ShapeDtypeStruct((windows, 47 * PER, refs), BF16),
            jax.ShapeDtypeStruct((3, windows, 19 * PER, refs), BF16),
        ],
        scratch_shapes=[pltpu.VMEM((2, PH, total // PH + 16, 128), F32)],
        compiler_params=pltpu.CompilerParams(vmem_limit_bytes=16 * 2**20),
        cost_estimate=pl.CostEstimate(flops=1000, bytes_accessed=1000, transcendentals=0),
    )(me[None], placed, placed_c)
    halves = [first_half, phases(after(series_x, shifted_refs), series_xc)]
    out = pl.pallas_call(
        functools.partial(corr_kernel, windows=windows, scale=1.0 / math.sqrt(total)),
        grid=(8,),
        in_specs=[vmem] * 4,
        out_specs=pl.BlockSpec((1, 4, 1, chan_rows, refs), lambda i: (i // 4, 0, i % 4, 0, 0)),
        out_shape=jax.ShapeDtypeStruct((2, 4, 4, chan_rows, refs), BF16),
        scratch_shapes=[pltpu.VMEM((3, windows, 19 * PER, refs), BF16)],
        compiler_params=pltpu.CompilerParams(vmem_limit_bytes=28 * 2**20),
        cost_estimate=pl.CostEstimate(flops=15 * 10**9, bytes_accessed=2 * 10**7, transcendentals=0),
    )(shifted_refs, differences, *halves)
    return out.reshape(lags_dev, chan_rows, refs)


def solution(mesh):
    in_specs = (P("chan", "tm"), P())
    out_specs = P("tm", "chan", None)
    sizes = (mesh.shape["chan"], mesh.shape["tm"])
    body = block_shards if sizes == (8, 4) else general_shards
    return jax.shard_map(body, mesh=mesh, in_specs=in_specs, out_specs=out_specs, check_vma=False)
```

```python
import functools
import math

import jax
import jax.numpy as jnp
from jax import lax
from jax.experimental import pallas as pl
from jax.experimental.pallas import tpu as pltpu
from jax.sharding import PartitionSpec as P

LAGS = 128
POOL = 32
BF16 = jnp.bfloat16
F32 = jnp.float32


def dot(a, b):
    return jnp.dot(a, b, preferred_element_type=F32)


def shifted(array, axis, by):
    size = lax.axis_size(axis)
    pairs = [(i, i + by) for i in range(size) if 0 <= i + by < size]
    return lax.ppermute(array, axis, pairs)


def lag_block(extended_rows, ref_block, first_lag, time_len, scale_factor):
    offsets = first_lag + jnp.arange(8, dtype=jnp.int32)
    windows = jax.vmap(lambda offset: lax.dynamic_slice_in_dim(extended_rows, offset, time_len, 1))(
        offsets
    )
    return (
        jnp.einsum("jct,rt->jcr", windows, ref_block, preferred_element_type=jnp.float32)
        * scale_factor
    )


def general_shards(series, ref_list):
    chan_rows, time_len = series.shape
    ref_count = ref_list.shape[1]
    group_index = lax.axis_index("chan")
    my_list = lax.dynamic_index_in_dim(ref_list, group_index, 0, keepdims=False)
    gathered_all = lax.all_gather(series, "chan", axis=0, tiled=True)
    ref_rows = jnp.take(gathered_all, my_list, axis=0)
    lag_tail = shifted(series[:, :LAGS], "tm", -1)
    extended = jnp.concatenate([series, lag_tail], axis=1)
    scale_factor = 1.0 / math.sqrt(time_len * lax.axis_size("tm"))
    lags_dev = LAGS // lax.axis_size("tm")

    def lag_step(carry, block_index):
        return (carry, lag_block(extended, ref_rows, 8 * block_index, time_len, scale_factor))

    _, stacked = lax.scan(
        lag_step, None, jnp.arange(lax.axis_size("tm") * lags_dev // 8, dtype=jnp.int32)
    )
    return lax.psum_scatter(
        stacked.reshape(lax.axis_size("tm") * lags_dev, chan_rows, ref_count).astype(jnp.bfloat16),
        "tm",
        scatter_dimension=0,
        tiled=True,
    )


def ones_where(condition):
    return jnp.where(condition, 1.0, 0.0).astype(BF16)


def iota(shape, dim):
    return lax.broadcasted_iota(jnp.int32, shape, dim)


def nt_dot(a, b):
    return lax.dot_general(a, b, (((1,), (1,)), ((), ())), preferred_element_type=F32)


def marks_of(list_ref, highs):
    groups, width = list_ref.shape
    rows = [list_ref[g : g + 1, c : c + 128] for g in range(groups) for c in range(0, width, 128)]
    high = jnp.concatenate([ones_where(iota((highs, 128), 0) == (row >> 7)) for row in rows], axis=1)
    low = jnp.concatenate([ones_where(iota((128, 128), 0) == (row & 127)) for row in rows], axis=1)
    return high, low


def select_kernel(group_ref, list_hbm, s_hbm, pool_ref, pair_ref, list_ref, s_ref, rank_ref, sem):
    list_copy = pltpu.make_async_copy(list_hbm, list_ref, sem.at[0])
    list_copy.start()
    copy = pltpu.make_async_copy(s_hbm, s_ref, sem.at[1])
    copy.start()
    list_copy.wait()
    per = s_ref.shape[0] // 128
    highs = list_ref.shape[0] * per
    high, low = marks_of(list_ref, highs)
    named = nt_dot(high, low) > 0.5
    marks = ones_where(named)
    before = ones_where(iota((128, 128), 0) < iota((128, 128), 1))
    held = dot(marks, jnp.ones((128, 128), BF16)).astype(BF16)
    h_to, h_from = iota((highs, highs), 0), iota((highs, highs), 1)
    earlier = ones_where((h_to // per == h_from // per) & (h_from < h_to))
    rank_ref[...] = jnp.where(named, dot(marks, before) + dot(earlier, held), -1.0)
    slot = iota((POOL, 128), 0).astype(F32)
    picks = [
        ones_where(jnp.broadcast_to(rank_ref[pl.ds(group_ref[0] * per + h, 1), :], (POOL, 128)) == slot)
        for h in range(per)
    ]
    copy.wait()
    rows = dot(jnp.concatenate(picks, axis=1), s_ref[...]).astype(BF16)
    pool_ref[...] = rows
    pair_ref[:POOL] = rows
    pair_ref[POOL:] = jnp.zeros_like(rows)


def order_kernel(group_ref, list_ref, order_ref, *, per):
    groups, width = list_ref.shape
    highs = groups * per
    own = group_ref[0]
    high, low = marks_of(list_ref, highs)
    marks = ones_where(nt_dot(low, high) > 0.5)
    after = ones_where(iota((128, 128), 1) < iota((128, 128), 0))
    held = dot(jnp.ones((128, 128), BF16), marks).astype(BF16)
    h_from, h_to = iota((highs, highs), 0), iota((highs, highs), 1)
    earlier = ones_where((h_to // per == h_from // per) & (h_from < h_to))
    rank = dot(after, marks) + dot(held, earlier)
    place = rank + (POOL * ((iota((128, highs), 1) // per) ^ own)).astype(F32)
    mine = list_ref[pl.ds(own, 1), :]
    mine_high = ones_where(iota((highs, width), 0) == (mine >> 7))
    mine_low = jnp.where(iota((128, width), 0) == (mine & 127), 1.0, 0.0)
    at = jnp.sum(dot(place.astype(BF16), mine_high) * mine_low, axis=0, keepdims=True)
    order_ref[...] = ones_where(iota(order_ref.shape, 0).astype(F32) == at)


PH = 16
WIN = 512
PER = WIN // PH
QUARTER = WIN // 4
COMBOS = ((0, 0), (1, 0), (1, 4), (2, 0), (3, 0), (3, 4), (2, 8), (3, 8), (3, 12))


def series_kernel(core_ref, mine_ref, other_ref, out_ref, raw, sem):
    time_len = mine_ref.shape[1]
    copies = [
        pltpu.make_async_copy(
            ref, raw.at[:, pl.ds(pl.multiple_of((core_ref[0] ^ e) * time_len, 128), time_len)], sem.at[e]
        )
        for e, ref in enumerate((mine_ref, other_ref))
    ]
    for copy in copies:
        copy.start()
    at, to = iota((WIN, WIN), 0), iota((WIN, WIN), 1)
    turn = ones_where(at == PH * (to & (PER - 1)) + to // PER)
    for copy in copies:
        copy.wait()
    for b in range(raw.shape[1] // WIN):
        turned = dot(raw[:, b * WIN : (b + 1) * WIN], turn)
        t = [turned[:, QUARTER * g : QUARTER * (g + 1)] for g in range(4)]
        u0, u1 = t[0] + t[2], t[1] + t[3]
        sums = (u0 + u1, u1, -u0, t[2] + t[3], t[3], -t[2], -(t[0] + t[1]), -t[1], t[0])
        for i, value in enumerate(sums):
            out_ref[i, :, b * QUARTER : (b + 1) * QUARTER] = value.astype(BF16)


def refs_kernel(order_ref, *refs):
    *pieces, out_ref = refs
    time_len = pieces[0].shape[1]
    at, to = iota((256, 256), 0), iota((256, 256), 1)
    turn = ones_where(to == PH * (at & 15) + (at >> 4))
    blocks = [(x, b) for x in range(2) for b in range(time_len // 256)]
    turned = []
    for x, b in blocks:
        block = [piece[POOL * x : POOL * (x + 1), 256 * b : 256 * (b + 1)] for piece in pieces]
        turned.append(nt_dot(turn, jnp.concatenate(block, axis=0)).astype(BF16))
    placed = dot(jnp.concatenate(turned, axis=0), order_ref[...]).astype(BF16)
    for i, (x, b) in enumerate(blocks):
        for p in range(PH):
            out_ref[x, p, 16 * b : 16 * (b + 1), :] = placed[256 * i + 16 * p : 256 * i + 16 * (p + 1)]


def slab(idx):
    return pl.ds(pl.multiple_of(idx * PER, PER), PER)


def make(xr, idx, rv, base, which, windows_of):
    for b in windows_of:
        x0, x4, x8, x12 = (xr[b, slab(idx + o), :] for o in (0, 4, 8, 12))
        f0 = x4 - x0
        if 0 in which:
            rv[0, b, slab(idx - base), :] = f0
        if 1 in which:
            rv[1, b, slab(idx - base), :] = x8 - x0
        rv[2, b, slab(idx - base), :] = (x12 - x8) - f0


def lag_kernel(tm_ref, mine_ref, other_ref, xr, rv0, xf):
    me = tm_ref[0]
    windows = xr.shape[0]
    half_w = windows // 2
    block_rows = mine_ref.shape[2]
    for h in range(2):
        lanes = slice(128 * h, 128 * h + 128)
        for p in range(PH):
            xf[h, p, 0:8, :] = jnp.zeros((8, 128), F32)
            for c, ref in enumerate((mine_ref, other_ref)):
                for x in range(2):
                    row = pl.multiple_of(8 + block_rows * (me ^ (c + 2 * x)), 8)
                    xf[h, p, pl.ds(row, block_rows), :] = ref[x, p, :, lanes].astype(F32)

    @pl.loop(0, 47, unroll=True)
    def _(idx):
        k = idx - 31
        for b in range(windows):
            half = (me >> 1) ^ (b // half_w)
            row = 8 + PER * (half_w * half + b % half_w) + (k >> 4) - 2 * me
            for h in range(2):
                xr[b, slab(idx), 128 * h : 128 * h + 128] = xf[h, k & 15, pl.ds(row, PER), :].astype(BF16)

    for low, high, which in ((24, 35, (0, 1)), (20, 24, (1,)), (16, 20, ())):

        @pl.loop(low, high, unroll=True)
        def _(idx):
            make(xr, idx, rv0, 16, which, range(windows))


def corr_kernel(xr, rv0, *refs, windows, scale):
    *halves, out_ref, rv1 = refs
    step = pl.program_id(0)

    def products(rv, beside):
        first = 15 - (step & 3)

        def product(i):
            v, off = COMBOS[i]
            if v == 0:
                rows = pl.ds(pl.multiple_of((first + 16 - 16 * (step >> 2)) * PER, PER), 4 * PER)
                parts = [xr[b, rows, :] for b in range(windows)]
            else:
                rows = pl.ds(pl.multiple_of((first - off) * PER, PER), 4 * PER)
                parts = [rv[v - 1, b, rows, :] for b in range(windows)]
            beside(i)
            return dot(jnp.concatenate([half[i] for half in halves], axis=1), jnp.concatenate(parts, axis=0))

        p = [product(i) for i in range(9)]
        w0, w1 = p[0] + p[3], p[0] + p[6]
        for at, value in enumerate((w0 + (p[1] + p[4]), w0 + (p[2] + p[5]), w1 + (p[1] + p[7]), w1 + (p[2] + p[8]))):
            out_ref[0, at, 0] = (scale * value).astype(BF16)

    @pl.when(step < 4)
    def _():
        def beside(i):
            for n in range(i, 5 * windows, 9):
                make(xr, jnp.maximum(18 - 5 * step - n // windows, 0), rv1, 0, (0, 1), (n % windows,))

        products(rv0, beside)

    @pl.when(step >= 4)
    def _():
        products(rv1, lambda i: None)


def flip(array, axis, by):
    return lax.ppermute(array, axis, [(i, i ^ by) for i in range(lax.axis_size(axis))])


def after(array, *others):
    return lax.optimization_barrier((array, *others))[0]


def block_shards(series, ref_list):
    chan_rows, time_len = series.shape
    groups, refs = ref_list.shape
    n_tm = lax.axis_size("tm")
    total = time_len * n_tm
    lags_dev = LAGS // n_tm
    group = lax.axis_index("chan").astype(jnp.int32)
    me = lax.axis_index("tm").astype(jnp.int32)
    smem = pl.BlockSpec(memory_space=pltpu.SMEM)
    vmem = pl.BlockSpec(memory_space=pltpu.VMEM)
    hbm = pl.BlockSpec(memory_space=pltpu.HBM)
    anywhere = pl.BlockSpec(memory_space=pl.ANY)
    small = pltpu.CompilerParams(vmem_limit_bytes=12 * 2**20)
    own_pool, pair = pl.pallas_call(
        select_kernel,
        in_specs=[smem, hbm, hbm],
        out_specs=[vmem, vmem],
        out_shape=[jax.ShapeDtypeStruct((rows, time_len), BF16) for rows in (POOL, 2 * POOL)],
        scratch_shapes=[
            pltpu.VMEM((groups, refs), jnp.int32),
            pltpu.VMEM((chan_rows, time_len), BF16),
            pltpu.VMEM((groups * chan_rows // 128, 128), F32),
            pltpu.SemaphoreType.DMA((2,)),
        ],
        compiler_params=pltpu.CompilerParams(vmem_limit_bytes=48 * 2**20),
    )(group[None], ref_list, series)
    pool_x = flip(own_pool, "tm", 2)
    order = pl.pallas_call(
        functools.partial(order_kernel, per=chan_rows // 128),
        in_specs=[smem, vmem],
        out_specs=vmem,
        out_shape=jax.ShapeDtypeStruct((groups * POOL, refs), BF16),
        compiler_params=small,
        cost_estimate=pl.CostEstimate(flops=10**9, bytes_accessed=10**6, transcendentals=0),
    )(group[None], after(ref_list, own_pool))
    series_c = flip(after(series, own_pool), "tm", 1)
    pair = lax.dynamic_update_slice(after(pair, order, series_c), pool_x, (POOL, 0))
    series_x = flip(after(series, pool_x, order), "tm", 2)
    along_z = [pair, flip(pair, "chan", 2), flip(pair, "chan", 4)]
    along_z.append(flip(along_z[2], "chan", 2))
    pool = []
    for piece in along_z:
        pool += [piece, flip(piece, "chan", 1)]

    def phases(mine, other):
        return pl.pallas_call(
            series_kernel,
            in_specs=[smem, hbm, hbm],
            out_specs=vmem,
            out_shape=jax.ShapeDtypeStruct((9, chan_rows, time_len // 2), BF16),
            scratch_shapes=[pltpu.VMEM((chan_rows, 2 * time_len), BF16), pltpu.SemaphoreType.DMA((2,))],
            compiler_params=pltpu.CompilerParams(vmem_limit_bytes=16 * 2**20),
            cost_estimate=pl.CostEstimate(
                flops=1000, bytes_accessed=1000, transcendentals=0
            ),
        )((me & 1)[None], mine, other)

    first_half = phases(series, series_c)
    placed = pl.pallas_call(
        refs_kernel,
        in_specs=[vmem] * (1 + len(pool)),
        out_specs=vmem,
        out_shape=jax.ShapeDtypeStruct((2, PH, time_len // PH, refs), BF16),
        compiler_params=small,
        cost_estimate=pl.CostEstimate(flops=8 * 10**8, bytes_accessed=10**6, transcendentals=0),
    )(after(order, first_half), *pool)
    placed_c = flip(placed, "tm", 1)
    series_xc = flip(after(series_x, placed), "tm", 1)
    windows = total // WIN
    shifted_refs, differences = pl.pallas_call(
        lag_kernel,
        in_specs=[smem, vmem, vmem],
        out_specs=[vmem] * 2,
        out_shape=[
            jax.ShapeDtypeStruct((windows, 47 * PER, refs), BF16),
            jax.ShapeDtypeStruct((3, windows, 19 * PER, refs), BF16),
        ],
        scratch_shapes=[pltpu.VMEM((2, PH, total // PH + 16, 128), F32)],
        compiler_params=pltpu.CompilerParams(vmem_limit_bytes=16 * 2**20),
        cost_estimate=pl.CostEstimate(flops=1000, bytes_accessed=1000, transcendentals=0),
    )(me[None], placed, placed_c)
    halves = [first_half, phases(after(series_x, shifted_refs), series_xc)]
    out = pl.pallas_call(
        functools.partial(corr_kernel, windows=windows, scale=1.0 / math.sqrt(total)),
        grid=(8,),
        in_specs=[vmem] * 4,
        out_specs=pl.BlockSpec((1, 4, 1, chan_rows, refs), lambda i: (i // 4, 0, i % 4, 0, 0)),
        out_shape=jax.ShapeDtypeStruct((2, 4, 4, chan_rows, refs), BF16),
        scratch_shapes=[pltpu.VMEM((3, windows, 19 * PER, refs), BF16)],
        compiler_params=pltpu.CompilerParams(vmem_limit_bytes=28 * 2**20),
        cost_estimate=pl.CostEstimate(flops=15 * 10**9, bytes_accessed=2 * 10**7, transcendentals=0),
    )(shifted_refs, differences, *halves)
    return out.reshape(lags_dev, chan_rows, refs)


def solution(mesh):
    in_specs = (P("chan", "tm"), P())
    out_specs = P("tm", "chan", None)
    sizes = (mesh.shape["chan"], mesh.shape["tm"])
    body = block_shards if sizes == (8, 4) else general_shards
    return jax.shard_map(body, mesh=mesh, in_specs=in_specs, out_specs=out_specs, check_vma=False)
```

```python
import functools
import math

import jax
import jax.numpy as jnp
from jax import lax
from jax.experimental import pallas as pl
from jax.experimental.pallas import tpu as pltpu
from jax.sharding import PartitionSpec as P

LAGS = 128
POOL = 32
BF16 = jnp.bfloat16
F32 = jnp.float32


def dot(a, b):
    return jnp.dot(a, b, preferred_element_type=F32)


def shifted(array, axis, by):
    size = lax.axis_size(axis)
    pairs = [(i, i + by) for i in range(size) if 0 <= i + by < size]
    return lax.ppermute(array, axis, pairs)


def lag_block(extended_rows, ref_block, first_lag, time_len, scale_factor):
    offsets = first_lag + jnp.arange(8, dtype=jnp.int32)
    windows = jax.vmap(lambda offset: lax.dynamic_slice_in_dim(extended_rows, offset, time_len, 1))(
        offsets
    )
    return (
        jnp.einsum("jct,rt->jcr", windows, ref_block, preferred_element_type=jnp.float32)
        * scale_factor
    )


def general_shards(series, ref_list):
    chan_rows, time_len = series.shape
    ref_count = ref_list.shape[1]
    group_index = lax.axis_index("chan")
    my_list = lax.dynamic_index_in_dim(ref_list, group_index, 0, keepdims=False)
    gathered_all = lax.all_gather(series, "chan", axis=0, tiled=True)
    ref_rows = jnp.take(gathered_all, my_list, axis=0)
    lag_tail = shifted(series[:, :LAGS], "tm", -1)
    extended = jnp.concatenate([series, lag_tail], axis=1)
    scale_factor = 1.0 / math.sqrt(time_len * lax.axis_size("tm"))
    lags_dev = LAGS // lax.axis_size("tm")

    def lag_step(carry, block_index):
        return (carry, lag_block(extended, ref_rows, 8 * block_index, time_len, scale_factor))

    _, stacked = lax.scan(
        lag_step, None, jnp.arange(lax.axis_size("tm") * lags_dev // 8, dtype=jnp.int32)
    )
    return lax.psum_scatter(
        stacked.reshape(lax.axis_size("tm") * lags_dev, chan_rows, ref_count).astype(jnp.bfloat16),
        "tm",
        scatter_dimension=0,
        tiled=True,
    )


def ones_where(condition):
    return jnp.where(condition, 1.0, 0.0).astype(BF16)


def iota(shape, dim):
    return lax.broadcasted_iota(jnp.int32, shape, dim)


def nt_dot(a, b):
    return lax.dot_general(a, b, (((1,), (1,)), ((), ())), preferred_element_type=F32)


def marks_of(list_ref, highs):
    groups, width = list_ref.shape
    rows = [list_ref[g : g + 1, c : c + 128] for g in range(groups) for c in range(0, width, 128)]
    high = jnp.concatenate([ones_where(iota((highs, 128), 0) == (row >> 7)) for row in rows], axis=1)
    low = jnp.concatenate([ones_where(iota((128, 128), 0) == (row & 127)) for row in rows], axis=1)
    return high, low


def select_kernel(group_ref, list_hbm, s_hbm, pool_ref, pair_ref, list_ref, s_ref, rank_ref, sem):
    list_copy = pltpu.make_async_copy(list_hbm, list_ref, sem.at[0])
    list_copy.start()
    copy = pltpu.make_async_copy(s_hbm, s_ref, sem.at[1])
    copy.start()
    list_copy.wait()
    per = s_ref.shape[0] // 128
    highs = list_ref.shape[0] * per
    high, low = marks_of(list_ref, highs)
    named = nt_dot(high, low) > 0.5
    marks = ones_where(named)
    before = ones_where(iota((128, 128), 0) < iota((128, 128), 1))
    held = dot(marks, jnp.ones((128, 128), BF16)).astype(BF16)
    h_to, h_from = iota((highs, highs), 0), iota((highs, highs), 1)
    earlier = ones_where((h_to // per == h_from // per) & (h_from < h_to))
    rank_ref[...] = jnp.where(named, dot(marks, before) + dot(earlier, held), -1.0)
    slot = iota((POOL, 128), 0).astype(F32)
    picks = [
        ones_where(jnp.broadcast_to(rank_ref[pl.ds(group_ref[0] * per + h, 1), :], (POOL, 128)) == slot)
        for h in range(per)
    ]
    copy.wait()
    rows = dot(jnp.concatenate(picks, axis=1), s_ref[...]).astype(BF16)
    pool_ref[...] = rows
    pair_ref[:POOL] = rows
    pair_ref[POOL:] = jnp.zeros_like(rows)


def order_kernel(group_ref, list_ref, order_ref, *, per):
    groups, width = list_ref.shape
    highs = groups * per
    own = group_ref[0]
    high, low = marks_of(list_ref, highs)
    marks = ones_where(nt_dot(low, high) > 0.5)
    after = ones_where(iota((128, 128), 1) < iota((128, 128), 0))
    held = dot(jnp.ones((128, 128), BF16), marks).astype(BF16)
    h_from, h_to = iota((highs, highs), 0), iota((highs, highs), 1)
    earlier = ones_where((h_to // per == h_from // per) & (h_from < h_to))
    rank = dot(after, marks) + dot(held, earlier)
    place = rank + (POOL * ((iota((128, highs), 1) // per) ^ own)).astype(F32)
    mine = list_ref[pl.ds(own, 1), :]
    mine_high = ones_where(iota((highs, width), 0) == (mine >> 7))
    mine_low = jnp.where(iota((128, width), 0) == (mine & 127), 1.0, 0.0)
    at = jnp.sum(dot(place.astype(BF16), mine_high) * mine_low, axis=0, keepdims=True)
    order_ref[...] = ones_where(iota(order_ref.shape, 0).astype(F32) == at)


PH = 16
WIN = 512
PER = WIN // PH
QUARTER = WIN // 4
COMBOS = ((0, 0), (1, 0), (1, 4), (2, 0), (3, 0), (3, 4), (2, 8), (3, 8), (3, 12))


def series_kernel(core_ref, mine_ref, other_ref, out_ref, raw, sem):
    time_len = mine_ref.shape[1]
    copies = [
        pltpu.make_async_copy(
            ref, raw.at[:, pl.ds(pl.multiple_of((core_ref[0] ^ e) * time_len, 128), time_len)], sem.at[e]
        )
        for e, ref in enumerate((mine_ref, other_ref))
    ]
    for copy in copies:
        copy.start()
    at, to = iota((WIN, WIN), 0), iota((WIN, WIN), 1)
    turn = ones_where(at == PH * (to & (PER - 1)) + to // PER)
    for copy in copies:
        copy.wait()
    for b in range(raw.shape[1] // WIN):
        turned = dot(raw[:, b * WIN : (b + 1) * WIN], turn)
        t = [turned[:, QUARTER * g : QUARTER * (g + 1)] for g in range(4)]
        u0, u1 = t[0] + t[2], t[1] + t[3]
        sums = (u0 + u1, u1, -u0, t[2] + t[3], t[3], -t[2], -(t[0] + t[1]), -t[1], t[0])
        for i, value in enumerate(sums):
            out_ref[i, :, b * QUARTER : (b + 1) * QUARTER] = value.astype(BF16)


def refs_kernel(order_ref, *refs):
    *pieces, out_ref = refs
    time_len = pieces[0].shape[1]
    at, to = iota((256, 256), 0), iota((256, 256), 1)
    turn = ones_where(to == PH * (at & 15) + (at >> 4))
    blocks = [(x, b) for x in range(2) for b in range(time_len // 256)]
    turned = []
    for x, b in blocks:
        block = [piece[POOL * x : POOL * (x + 1), 256 * b : 256 * (b + 1)] for piece in pieces]
        turned.append(nt_dot(turn, jnp.concatenate(block, axis=0)).astype(BF16))
    placed = dot(jnp.concatenate(turned, axis=0), order_ref[...]).astype(BF16)
    for i, (x, b) in enumerate(blocks):
        for p in range(PH):
            out_ref[x, p, 16 * b : 16 * (b + 1), :] = placed[256 * i + 16 * p : 256 * i + 16 * (p + 1)]


def slab(idx):
    return pl.ds(pl.multiple_of(idx * PER, PER), PER)


def make(xr, idx, rv, base, which, windows_of):
    for b in windows_of:
        x0, x4, x8, x12 = (xr[b, slab(idx + o), :] for o in (0, 4, 8, 12))
        f0 = x4 - x0
        if 0 in which:
            rv[0, b, slab(idx - base), :] = f0
        if 1 in which:
            rv[1, b, slab(idx - base), :] = x8 - x0
        rv[2, b, slab(idx - base), :] = (x12 - x8) - f0


def lag_kernel(tm_ref, mine_ref, other_ref, xr, rv0, xf):
    me = tm_ref[0]
    windows = xr.shape[0]
    half_w = windows // 2
    block_rows = mine_ref.shape[2]
    for h in range(2):
        lanes = slice(128 * h, 128 * h + 128)
        for p in range(PH):
            xf[h, p, 0:8, :] = jnp.zeros((8, 128), F32)
            for c, ref in enumerate((mine_ref, other_ref)):
                for x in range(2):
                    row = pl.multiple_of(8 + block_rows * (me ^ (c + 2 * x)), 8)
                    xf[h, p, pl.ds(row, block_rows), :] = ref[x, p, :, lanes].astype(F32)

    @pl.loop(0, 47, unroll=True)
    def _(idx):
        k = idx - 31
        for b in range(windows):
            half = (me >> 1) ^ (b // half_w)
            row = 8 + PER * (half_w * half + b % half_w) + (k >> 4) - 2 * me
            for h in range(2):
                xr[b, slab(idx), 128 * h : 128 * h + 128] = xf[h, k & 15, pl.ds(row, PER), :].astype(BF16)

    for low, high, which in ((24, 35, (0, 1)), (20, 24, (1,)), (16, 20, ())):

        @pl.loop(low, high, unroll=True)
        def _(idx):
            make(xr, idx, rv0, 16, which, range(windows))


def corr_kernel(xr, rv0, *refs, windows, scale):
    *halves, out_ref, rv1 = refs
    step = pl.program_id(0)

    def products(rv, sub, beside):
        lag = 2 * step + sub
        first = 15 - (lag & 3)

        def product(i):
            v, off = COMBOS[i]
            if v == 0:
                rows = pl.ds(pl.multiple_of((first + 16 - 16 * (lag >> 2)) * PER, PER), 4 * PER)
                parts = [xr[b, rows, :] for b in range(windows)]
            else:
                rows = pl.ds(pl.multiple_of((first - off) * PER, PER), 4 * PER)
                parts = [rv[v - 1, b, rows, :] for b in range(windows)]
            beside(i)
            return dot(jnp.concatenate([half[i] for half in halves], axis=1), jnp.concatenate(parts, axis=0))

        p = [product(i) for i in range(9)]
        w0, w1 = p[0] + p[3], p[0] + p[6]
        for at, value in enumerate((w0 + (p[1] + p[4]), w0 + (p[2] + p[5]), w1 + (p[1] + p[7]), w1 + (p[2] + p[8]))):
            out_ref[0, at, sub] = (scale * value).astype(BF16)

    @pl.when(step < 2)
    def _():
        def beside(i):
            for n in range(i, 10 * windows, 18):
                make(xr, jnp.maximum(18 - 10 * step - n // windows, 0), rv1, 0, (0, 1), (n % windows,))

        products(rv0, 0, beside)
        products(rv0, 1, lambda i: beside(i + 9))

    @pl.when(step >= 2)
    def _():
        products(rv1, 0, lambda i: None)
        products(rv1, 1, lambda i: None)


def flip(array, axis, by):
    return lax.ppermute(array, axis, [(i, i ^ by) for i in range(lax.axis_size(axis))])


def after(array, *others):
    return lax.optimization_barrier((array, *others))[0]


def block_shards(series, ref_list):
    chan_rows, time_len = series.shape
    groups, refs = ref_list.shape
    n_tm = lax.axis_size("tm")
    total = time_len * n_tm
    lags_dev = LAGS // n_tm
    group = lax.axis_index("chan").astype(jnp.int32)
    me = lax.axis_index("tm").astype(jnp.int32)
    smem = pl.BlockSpec(memory_space=pltpu.SMEM)
    vmem = pl.BlockSpec(memory_space=pltpu.VMEM)
    hbm = pl.BlockSpec(memory_space=pltpu.HBM)
    anywhere = pl.BlockSpec(memory_space=pl.ANY)
    small = pltpu.CompilerParams(vmem_limit_bytes=12 * 2**20)
    own_pool, pair = pl.pallas_call(
        select_kernel,
        in_specs=[smem, hbm, hbm],
        out_specs=[vmem, vmem],
        out_shape=[jax.ShapeDtypeStruct((rows, time_len), BF16) for rows in (POOL, 2 * POOL)],
        scratch_shapes=[
            pltpu.VMEM((groups, refs), jnp.int32),
            pltpu.VMEM((chan_rows, time_len), BF16),
            pltpu.VMEM((groups * chan_rows // 128, 128), F32),
            pltpu.SemaphoreType.DMA((2,)),
        ],
        compiler_params=pltpu.CompilerParams(vmem_limit_bytes=48 * 2**20),
    )(group[None], ref_list, series)
    pool_x = flip(own_pool, "tm", 2)
    order = pl.pallas_call(
        functools.partial(order_kernel, per=chan_rows // 128),
        in_specs=[smem, vmem],
        out_specs=vmem,
        out_shape=jax.ShapeDtypeStruct((groups * POOL, refs), BF16),
        compiler_params=small,
        cost_estimate=pl.CostEstimate(flops=10**9, bytes_accessed=10**6, transcendentals=0),
    )(group[None], after(ref_list, own_pool))
    series_c = flip(after(series, own_pool), "tm", 1)
    pair = lax.dynamic_update_slice(after(pair, order, series_c), pool_x, (POOL, 0))
    series_x = flip(after(series, pool_x, order), "tm", 2)
    along_z = [pair, flip(pair, "chan", 2), flip(pair, "chan", 4)]
    along_z.append(flip(along_z[2], "chan", 2))
    pool = []
    for piece in along_z:
        pool += [piece, flip(piece, "chan", 1)]

    def phases(mine, other):
        return pl.pallas_call(
            series_kernel,
            in_specs=[smem, hbm, hbm],
            out_specs=vmem,
            out_shape=jax.ShapeDtypeStruct((9, chan_rows, time_len // 2), BF16),
            scratch_shapes=[pltpu.VMEM((chan_rows, 2 * time_len), BF16), pltpu.SemaphoreType.DMA((2,))],
            compiler_params=pltpu.CompilerParams(vmem_limit_bytes=16 * 2**20),
            cost_estimate=pl.CostEstimate(
                flops=1000, bytes_accessed=1000, transcendentals=0
            ),
        )((me & 1)[None], mine, other)

    first_half = phases(series, series_c)
    placed = pl.pallas_call(
        refs_kernel,
        in_specs=[vmem] * (1 + len(pool)),
        out_specs=vmem,
        out_shape=jax.ShapeDtypeStruct((2, PH, time_len // PH, refs), BF16),
        compiler_params=small,
        cost_estimate=pl.CostEstimate(flops=8 * 10**8, bytes_accessed=10**6, transcendentals=0),
    )(after(order, first_half), *pool)
    placed_c = flip(placed, "tm", 1)
    series_xc = flip(after(series_x, placed), "tm", 1)
    windows = total // WIN
    shifted_refs, differences = pl.pallas_call(
        lag_kernel,
        in_specs=[smem, vmem, vmem],
        out_specs=[vmem] * 2,
        out_shape=[
            jax.ShapeDtypeStruct((windows, 47 * PER, refs), BF16),
            jax.ShapeDtypeStruct((3, windows, 19 * PER, refs), BF16),
        ],
        scratch_shapes=[pltpu.VMEM((2, PH, total // PH + 16, 128), F32)],
        compiler_params=pltpu.CompilerParams(vmem_limit_bytes=16 * 2**20),
        cost_estimate=pl.CostEstimate(flops=1000, bytes_accessed=1000, transcendentals=0),
    )(me[None], placed, placed_c)
    halves = [first_half, phases(after(series_x, shifted_refs), series_xc)]
    out = pl.pallas_call(
        functools.partial(corr_kernel, windows=windows, scale=1.0 / math.sqrt(total)),
        grid=(4,),
        in_specs=[vmem] * 4,
        out_specs=pl.BlockSpec((1, 4, 2, chan_rows, refs), lambda i: (i // 2, 0, i % 2, 0, 0)),
        out_shape=jax.ShapeDtypeStruct((2, 4, 4, chan_rows, refs), BF16),
        scratch_shapes=[pltpu.VMEM((3, windows, 19 * PER, refs), BF16)],
        compiler_params=pltpu.CompilerParams(vmem_limit_bytes=28 * 2**20),
        cost_estimate=pl.CostEstimate(flops=15 * 10**9, bytes_accessed=2 * 10**7, transcendentals=0),
    )(shifted_refs, differences, *halves)
    return out.reshape(lags_dev, chan_rows, refs)


def solution(mesh):
    in_specs = (P("chan", "tm"), P())
    out_specs = P("tm", "chan", None)
    sizes = (mesh.shape["chan"], mesh.shape["tm"])
    body = block_shards if sizes == (8, 4) else general_shards
    return jax.shard_map(body, mesh=mesh, in_specs=in_specs, out_specs=out_specs, check_vma=False)
```
